32 devices in a mesh: groups: 2 (over y), row: 4 (over z), col: 4 (over x, core).
Axes of the slice: x: 2, y: 2, z: 4, core: 2. Of those that a mesh axis runs over, the one named last changes fastest.
Arguments:
- vectors: float32 [4, 256, 16384], P('groups', 'col', 'row'), parts along dimension 0, may hold values from -0.046875 to 0.046875
- factors: float32 [4, 256, 256], P('groups'), parts along dimension 0, as said below
- eigvecs: float32 [32768, 2048], P(('groups', 'row'), 'col'), parts along dimension 0, may hold values from -6 to 6
Outputs:
- transformed: float32 [32768, 2048], P(('groups', 'row'), 'col'), parts along dimension 0
The draws below stay inside these ranges and needn't reach their ends.
There are 2 independent parts, one for each index of `groups`. The reference program is written for one: setup_inputs(seed, part) draws one part's arguments, and reference() takes and returns one part's arrays. A program takes and returns all parts, laid end to end along the dimension named above; each array names one. Nothing has to cross between parts.
Inputs may be any that keep to these rules, and one draw needn't show every extreme that they name: factors[k] is upper triangular with a positive diagonal.
All inputs are finite; a program needn't handle non-finite values.
Results may differ from the reference program's by a relative error of at most 0.0001.
Values sent between devices are 32-bit elements; how exact they have to be, the bound alone decides.
No kernel may reach another device: no remote copies, remote signals or barrier semaphores. Data moves between devices by JAX's collectives and lax.ppermute only.
A program may use at most 128 MiB of HBM per device.

```python
import jax
import jax.numpy as jnp
from jax import lax

M = 16384
B = 256
NC = 2048


def draw_factors(key, part):
    key = jax.random.fold_in(key, 7)
    first, second = jax.random.split(key)
    upper = jax.random.normal(first, (2, B, B), jnp.float32) * (0.5 / B ** 0.5)
    diagonal = jnp.exp(jax.random.uniform(second, (2, B), jnp.float32, jnp.log(0.5), jnp.log(1.5)))
    return jnp.triu(upper, 1) + diagonal[:, :, None] * jnp.eye(B, dtype=jnp.float32)[None]


def steps_of(own_key, dims, shards, least, top_value):
    def one(dim, blocks):
        heights = jax.random.uniform(jax.random.fold_in(jax.random.fold_in(own_key, 6), dim), (blocks,), jnp.float32, least / len(shards), top_value / len(shards))
        return jnp.repeat(jnp.exp(heights), dims[dim] // blocks).reshape((-1,) + (1,) * (len(dims) - dim - 1))

    gain = one(*shards[0])
    for cut in shards[1:]:
        gain = gain * one(*cut)
    return gain


def gaussian(key, extent, scale, most, shards=(), kind=jnp.bfloat16):
    level = steps_of(key, extent, shards, -0.22, 0.18) if shards else 1.0
    entries = jax.random.normal(key, extent, jnp.float32) * scale * level
    return jnp.minimum(jnp.maximum(entries, -most), most).astype(kind)


def setup_inputs(seed: int = 0, part: int = 0) -> dict:
    splits = jax.random.split(jax.random.key(seed), 4)
    own_keys = jax.random.split(jax.random.fold_in(splits[3], part), 4)
    vectors = gaussian(own_keys[0], (2, B, M), M ** -0.5, 0.046875, ((1, 4), (2, 4)), jnp.float32)
    factors = draw_factors(jax.random.fold_in(jax.random.fold_in(splits[3], part), 71), part)
    eigvecs = gaussian(own_keys[2], (M, NC), 1.0, 6.0, ((0, 4), (1, 4)), jnp.float32)
    return {"vectors": vectors, "factors": factors, "eigvecs": eigvecs}


HIGH = lax.Precision.HIGHEST


def masked(block, start):
    along = lax.broadcasted_iota(jnp.int32, block.shape, 0)
    across = lax.broadcasted_iota(jnp.int32, block.shape, 1)
    return jnp.where(across >= along + start, block, jnp.zeros_like(block))


def reference(vectors, factors, eigvecs):
    current = eigvecs
    for index in (1, 0):
        reflector = masked(vectors[index], index * B)
        project = jnp.dot(reflector, current, precision=HIGH)
        scaled = jnp.dot(factors[index], project, precision=HIGH)
        current = current - jnp.dot(reflector.T, scaled, precision=HIGH)
    return current
```

```python
import jax
import jax.numpy as jnp
from jax import lax
from jax.sharding import PartitionSpec as P

HIGH = lax.Precision.HIGH
PIECES = (((1, 0, 64),), ((0, 0, 32),), ((0, 32, 48),), ((0, 48, 64),))


def mm(a, b):
    return jnp.dot(a, b, precision=HIGH)


def mmt(a, b):
    return lax.dot_general(a, b, (((1,), (1,)), ((), ())), precision=HIGH)


def tmm(a, b):
    return lax.dot_general(a, b, (((0,), (0,)), ((), ())), precision=HIGH)


def make_local(chips, rows):
    cols = 2 * chips

    def core_swap(value):
        return lax.ppermute(value, "col", [(i, i ^ 1) for i in range(cols)])

    def from_chip(value, step):
        return lax.ppermute(value, "col", [((i + 2 * step) % cols, i) for i in range(cols)])

    def row_sum(value):
        step = 1
        while step < rows:
            value = value + lax.ppermute(value, "row", [(i, i ^ step) for i in range(rows)])
            step *= 2
        return value

    def local(vectors, factors, eigvecs):
        share, here = vectors.shape[1:]
        col = lax.axis_index("col")
        width = share * cols
        first = lax.axis_index("row") * here
        along = lax.broadcasted_iota(jnp.int32, vectors.shape, 1) + col * share
        along = along + lax.broadcasted_iota(jnp.int32, vectors.shape, 0) * width
        across = lax.broadcasted_iota(jnp.int32, vectors.shape, 2) + first
        mine = jnp.where(across >= along, vectors, 0.0)

        def reorder(value):
            value = value.reshape(chips, 2, share, chips, 2, share)
            chip, core = col // 2, col % 2
            value = jnp.roll(jnp.roll(value, -chip, 0), -chip, 3)
            value = jnp.roll(jnp.roll(value, core, 1), core, 4)
            return value.reshape(width, width)

        t0, t1 = reorder(factors[0]), reorder(factors[1])

        pieces = []
        for (piece,) in PIECES:
            block, low, high = piece
            low, high = low * share // 64, high * share // 64
            for step in range(1, chips):
                pieces.append((block, step, low, high, from_chip(mine[block, low:high], step)))
        sib = core_swap(mine)
        own = {k: jnp.concatenate([mine[k], sib[k]]) for k in (0, 1)}
        both = jnp.concatenate([own[1], own[0]])
        half = own[0].shape[0]
        mix = jnp.concatenate([mm(both, eigvecs), mmt(both, own[1])], axis=1)
        mix = lax.psum(mix, "row")
        nc = eigvecs.shape[1]
        p1 = [mix[:half, :nc]]
        p0 = [mix[half:, :nc]]
        gram = [mix[half:, nc:]]
        v1, v0 = [own[1]], [own[0]]
        ones = [p for p in pieces if p[0] == 1]
        zeros = [p for p in pieces if p[0] == 0]
        order0 = [(0, 0, 0, share)]
        for block, step, low, high, value in ones:
            value = jnp.concatenate([value, core_swap(value)])
            v1.append(value)
            part = jnp.concatenate([mm(value, eigvecs), mmt(own[0], value)], axis=1)
            part = row_sum(part)
            p1.append(part[:, :nc])
            gram.append(part[:, nc:])
        all1 = jnp.concatenate(v1)
        gram = [jnp.concatenate(gram, axis=1)]
        for block, step, low, high, value in zeros:
            value = jnp.concatenate([value, core_swap(value)])
            v0.append(value)
            part = jnp.concatenate([mm(value, eigvecs), mmt(value, all1)], axis=1)
            part = row_sum(part)
            p0.append(part[:, :nc])
            gram.append(part[:, nc:])
            order0.append((step, 0, low, high))
        s1 = mm(t1, jnp.concatenate(p1))
        current = eigvecs - tmm(all1, s1)
        t0 = t0.reshape(chips, 2, share, chips, 2, share)
        groups = [(0, 0, share)] + [(step, low, high) for _, step, low, high, _ in zeros]
        t0 = jnp.concatenate([t0[s, :, a:b].reshape(2 * (b - a), chips, 2, share) for s, a, b in groups])
        t0 = jnp.concatenate([t0[:, s, :, a:b].reshape(width, 2 * (b - a)) for s, a, b in groups], axis=1)
        p0 = [value - mm(g, s1) for value, g in zip(p0, gram)]
        s0 = mm(t0, jnp.concatenate(p0))
        return current - tmm(jnp.concatenate(v0), s0)

    return local


def solution(mesh):
    placed = (P("groups", "col", "row"), P("groups", None, None), P(("groups", "row"), "col"))
    local = make_local(mesh.shape["col"] // 2, mesh.shape["row"])
    return jax.shard_map(
        local, mesh=mesh, in_specs=placed, out_specs=P(("groups", "row"), "col"), check_vma=False
    )
```

```python
import functools

import jax
import jax.numpy as jnp
from jax import lax
from jax.experimental import pallas as pl
from jax.experimental.pallas import tpu as pltpu
from jax.sharding import PartitionSpec as P

F32, BF16 = jnp.float32, jnp.bfloat16
PIECES = ((1, 0, 32), (1, 32, 64), (0, 0, 40), (0, 40, 64))
NN = (((1,), (0,)), ((), ()))
NT = (((1,), (1,)), ((), ()))
TN = (((0,), (0,)), ((), ()))


def params(mib):
    return pltpu.CompilerParams(
        dimension_semantics=("arbitrary",), vmem_limit_bytes=mib * 1024 * 1024
    )


def whole(shape):
    return pl.BlockSpec(shape, lambda i: (0,) * len(shape))


def cost(flops, moved):
    return pl.CostEstimate(flops=flops, bytes_accessed=moved, transcendentals=0)


SCALARS = pl.BlockSpec(memory_space=pltpu.SMEM)


def split(value):
    high = value.astype(BF16)
    return high, (value - high.astype(F32)).astype(BF16)


def full_dot(a, b, dims=NN):
    return lax.dot_general(a, b, dims, precision=lax.Precision.HIGHEST, preferred_element_type=F32)


def three(vh, vl, b, dims):
    rows = vh.shape[0]
    bh, bl = split(b)
    first = lax.dot_general(jnp.concatenate([vh, vl]), bh, dims, preferred_element_type=F32)
    second = lax.dot_general(vh, bl, dims, preferred_element_type=F32)
    return first[:rows] + first[rows:] + second


def cut(where, vectors, pieces):
    _, share, here = vectors.shape
    step = min(here, 1024)

    def body(where_ref, in_ref, *outs):
        for (block, low, high), out in zip(pieces, outs):
            shape = (high - low, step)
            along = lax.broadcasted_iota(jnp.int32, shape, 0) + (where_ref[0] + low)
            across = lax.broadcasted_iota(jnp.int32, shape, 1) + (where_ref[1] + pl.program_id(0) * step)
            out[...] = jnp.where(across >= along + block * where_ref[2], in_ref[block, low:high], 0.0)

    return pl.pallas_call(
        body,
        grid=(here // step,),
        in_specs=[SCALARS, pl.BlockSpec((2, share, step), lambda i: (0, 0, i))],
        out_specs=[pl.BlockSpec((b - a, step), lambda i: (0, i)) for _, a, b in pieces],
        out_shape=[jax.ShapeDtypeStruct((b - a, here), F32) for _, a, b in pieces],
        compiler_params=params(16),
        cost_estimate=cost(0, 4 * vectors.size * 2),
        name="cut",
    )(where, vectors)


def project(rows, partners, eigvecs, bit=None):
    here, nc = eigvecs.shape
    step = min(here, 512)
    height = sum(r.shape[0] for r in rows)
    extra = sum(r.shape[0] for r in partners)
    steps = here // step

    def body(*refs):
        refs = list(refs)
        bit_ref = refs.pop(0) if bit is not None else None
        row_refs, partner_refs = refs[: len(rows)], refs[len(rows) : len(rows) + len(partners)]
        eig_ref = refs[len(rows) + len(partners)]
        outs, acc = refs[len(rows) + len(partners) + 1 : -1], refs[-1]
        k = pl.program_id(0)

        @pl.when(k == 0)
        def _():
            acc[...] = jnp.zeros_like(acc)

        vh, vl = split(jnp.concatenate([r[...] for r in row_refs]))
        acc[:, :nc] += three(vh, vl, eig_ref[...], NN)
        if partners:
            acc[:, nc:] += three(vh, vl, jnp.concatenate([r[...] for r in partner_refs]), NT)

        @pl.when(k == steps - 1)
        def _():
            if bit is None:
                outs[0][...] = acc[...]
            else:
                half = height // 2
                zero = bit_ref[0] == 0
                outs[0][...] = jnp.where(zero, acc[:half], acc[half:])
                outs[1][...] = jnp.where(zero, acc[half:], acc[:half])

    count = 1 if bit is None else 2
    shape = (height // count, nc + extra)
    return pl.pallas_call(
        body,
        grid=(steps,),
        in_specs=([] if bit is None else [SCALARS])
        + [pl.BlockSpec((r.shape[0], step), lambda i: (0, i)) for r in rows + partners]
        + [pl.BlockSpec((step, nc), lambda i: (i, 0))],
        out_specs=[whole(shape)] * count,
        out_shape=[jax.ShapeDtypeStruct(shape, F32)] * count,
        scratch_shapes=[pltpu.VMEM((height, nc + extra), F32)],
        compiler_params=params(32),
        cost_estimate=cost(6 * height * here * (nc + extra), 4 * (eigvecs.size + height * here)),
        name="project",
    )(*([] if bit is None else [bit]), *rows, *partners, eigvecs)


def turn(pieces):
    here = pieces[0].shape[1]
    step = min(here, 512)
    height = sum(r.shape[0] for r in pieces)

    def body(*refs):
        turned = jnp.concatenate([r[...] for r in refs[:-2]]).T
        high, low = split(turned)
        refs[-2][...] = high
        refs[-1][...] = low

    return pl.pallas_call(
        body,
        grid=(here // step,),
        in_specs=[pl.BlockSpec((r.shape[0], step), lambda i: (0, i)) for r in pieces],
        out_specs=[pl.BlockSpec((step, height), lambda i: (i, 0))] * 2,
        out_shape=[jax.ShapeDtypeStruct((here, height), BF16)] * 2,
        compiler_params=params(16),
        cost_estimate=cost(0, 8 * height * here),
        name="turn",
    )(*pieces)


def reorder(where, factors, share, chips, segments):
    width = factors.shape[1]

    def body(where_ref, in_ref, *outs):
        chip, core = where_ref[3], where_ref[4]
        for block, out in enumerate(outs):
            picks = []
            for step, other, low, high in segments[block]:
                at = (lax.rem(chip + step, chips) * 2 + (core + other) % 2) * share + low
                shape = (high - low, width)
                same = lax.broadcasted_iota(jnp.int32, shape, 1) == lax.broadcasted_iota(jnp.int32, shape, 0) + at
                picks.append(jnp.where(same, 1.0, 0.0))
            pick = jnp.concatenate(picks)
            out[...] = full_dot(full_dot(pick, in_ref[block]), pick, NT)

    return pl.pallas_call(
        body,
        grid=(1,),
        in_specs=[SCALARS, whole(factors.shape)],
        out_specs=[whole((width, width))] * 2,
        out_shape=[jax.ShapeDtypeStruct((width, width), F32)] * 2,
        compiler_params=params(16),
        cost_estimate=cost(48 * width**3, 8 * factors.size),
        name="reorder",
    )(where, factors)


def update(make, ins, factor, turned, current, with_scaled):
    here, nc = current.shape
    width = factor.shape[0]
    step = min(here, 512)

    def body(*refs):
        in_refs, rest = refs[: len(ins)], refs[len(ins) :]
        factor_ref, high_ref, low_ref, cur_ref = rest[:4]
        outs, (sh_ref, sl_ref) = rest[4:-2], rest[-2:]

        @pl.when(pl.program_id(0) == 0)
        def _():
            scaled = full_dot(factor_ref[...], make(*in_refs))
            sh_ref[...], sl_ref[...] = split(scaled)
            if with_scaled:
                outs[1][...] = scaled

        high, low = high_ref[...], low_ref[...]
        sh, sl = sh_ref[...], sl_ref[...]
        dot = functools.partial(jnp.dot, preferred_element_type=F32)
        outs[0][...] = cur_ref[...] - (dot(high, sh) + dot(high, sl) + dot(low, sh))

    def spec(value):
        return SCALARS if value.dtype == jnp.int32 else whole(value.shape)

    tall = pl.BlockSpec((step, width), lambda i: (i, 0))
    wide = pl.BlockSpec((step, nc), lambda i: (i, 0))
    out_specs, out_shape = [wide], [jax.ShapeDtypeStruct((here, nc), F32)]
    if with_scaled:
        out_specs.append(whole((width, nc)))
        out_shape.append(jax.ShapeDtypeStruct((width, nc), F32))
    return pl.pallas_call(
        body,
        grid=(here // step,),
        in_specs=[spec(v) for v in ins] + [whole(factor.shape), tall, tall, wide],
        out_specs=out_specs,
        out_shape=out_shape,
        scratch_shapes=[pltpu.VMEM((width, nc), BF16)] * 2,
        compiler_params=params(32),
        cost_estimate=cost(6 * here * width * nc, 4 * here * (2 * nc + width)),
        name="update",
    )(*ins, factor, *turned, current)


def make_local(chips, rows):
    cols = 2 * chips

    def core_swap(value):
        return lax.ppermute(value, "col", [(i, i ^ 1) for i in range(cols)])

    def from_chip(value, step):
        return lax.ppermute(value, "col", [((i + 2 * step) % cols, i) for i in range(cols)])

    def row_swap(value, step):
        return lax.ppermute(value, "row", [(i, i ^ step) for i in range(rows)])

    def row_sum(value, step=1):
        while step < rows:
            value = value + row_swap(value, step)
            step *= 2
        return value

    def halves_sum(keep, send):
        mine = row_sum(keep + row_swap(send, 1), 2)
        return mine, row_swap(mine, 1)

    def local(vectors, factors, eigvecs):
        share, here = vectors.shape[1:]
        nc = eigvecs.shape[1]
        width = share * cols
        half = 2 * share
        col, row = lax.axis_index("col"), lax.axis_index("row")
        where = jnp.stack([col * share, row * here, jnp.int32(width), col // 2, col % 2]).astype(jnp.int32)
        bit = (row % 2).astype(jnp.int32)[None]
        pieces = []
        for block, low, high in PIECES:
            low, high = low * share // 64 // 8 * 8, high * share // 64 // 8 * 8
            pieces.append((block, low, high))

        mine = cut(where, vectors, pieces)
        far = [(step, p, from_chip(m, step)) for p, m in zip(pieces, mine) for step in range(1, chips)]
        own, segments = {0: [], 1: []}, {0: [], 1: []}
        for (block, low, high), m in zip(pieces, mine):
            own[block] += [m, core_swap(m)]
            segments[block] += [(0, 0, low, high), (0, 1, low, high)]
        all_ones, all_zeros = list(own[1]), list(own[0])
        ones = [halves_sum(*project(own[1], own[0], eigvecs, bit))]
        own_zero = lax.psum(project(own[0], [], eigvecs)[0], "row")
        zeros = []
        for step, (block, low, high), value in far:
            pair = [value, core_swap(value)]
            segments[block] += [(step, 0, low, high), (step, 1, low, high)]
            if block == 1:
                all_ones += pair
                ones.append(halves_sum(*project(pair, own[0], eigvecs, bit)))
            else:
                all_zeros += pair
                zeros.append(row_sum(project(pair, all_ones, eigvecs)[0]))
        t0, t1 = reorder(where, factors, share, chips, segments)

        def joined(bit_ref, refs, columns):
            parts = []
            zero = bit_ref[0] == 0
            for a, b in zip(refs[::2], refs[1::2]):
                a, b = a[:, columns], b[:, columns]
                parts += [jnp.where(zero, a, b), jnp.where(zero, b, a)]
            return jnp.concatenate(parts)

        flat = [v for pair in ones for v in pair]

        def make_one(bit_ref, *refs):
            return joined(bit_ref, refs, slice(0, nc))

        def make_zero(bit_ref, scaled_ref, own_ref, *refs):
            ones_refs, zero_refs = refs[: len(flat)], refs[len(flat) :]
            scaled = scaled_ref[...]
            turned_gram = joined(bit_ref, ones_refs, slice(nc, nc + half))
            parts = [own_ref[...] - full_dot(turned_gram, scaled, TN)]
            later = jnp.concatenate([r[...] for r in zero_refs])
            parts.append(later[:, :nc] - full_dot(later[:, nc:], scaled))
            return jnp.concatenate(parts)

        current, scaled = update(make_one, [bit, *flat], t1, turn(all_ones), eigvecs, True)
        (out,) = update(make_zero, [bit, scaled, own_zero, *flat, *zeros], t0, turn(all_zeros), current, False)
        return out

    return local


def solution(mesh):
    placed = (P("groups", "col", "row"), P("groups", None, None), P(("groups", "row"), "col"))
    local = make_local(mesh.shape["col"] // 2, mesh.shape["row"])
    return jax.shard_map(
        local, mesh=mesh, in_specs=placed, out_specs=P(("groups", "row"), "col"), check_vma=False
    )
```

```python
import functools

import jax
import jax.numpy as jnp
from jax import lax
from jax.experimental import pallas as pl
from jax.experimental.pallas import tpu as pltpu
from jax.sharding import PartitionSpec as P

F32, BF16 = jnp.float32, jnp.bfloat16
PIECES = ((1, 0, 32), (1, 32, 64), (0, 0, 40), (0, 40, 64))
NN = (((1,), (0,)), ((), ()))
NT = (((1,), (1,)), ((), ()))
TN = (((0,), (0,)), ((), ()))


def params(mib):
    return pltpu.CompilerParams(
        dimension_semantics=("arbitrary",), vmem_limit_bytes=mib * 1024 * 1024
    )


def whole(shape):
    return pl.BlockSpec(shape, lambda i: (0,) * len(shape))


def cost(flops, moved):
    return pl.CostEstimate(flops=flops, bytes_accessed=moved, transcendentals=0)


ROOM = 56
SCALARS = pl.BlockSpec(memory_space=pltpu.SMEM)


def split(value):
    high = value.astype(BF16)
    return high, (value - high.astype(F32)).astype(BF16)


def strips(pieces, step):
    return [pl.BlockSpec((count, step), lambda i, at=at: (at, i)) for _, count, at in pieces]


def full_dot(a, b, dims=NN):
    return lax.dot_general(a, b, dims, precision=lax.Precision.HIGHEST, preferred_element_type=F32)


def three(vh, vl, b, dims):
    rows = vh.shape[0]
    bh, bl = split(b)
    first = lax.dot_general(jnp.concatenate([vh, vl]), bh, dims, preferred_element_type=F32)
    second = lax.dot_general(vh, bl, dims, preferred_element_type=F32)
    return first[:rows] + first[rows:] + second


def cut(where, vectors, after, rows, name):
    _, share, here = vectors.shape
    step = min(here, 1024)
    height = sum(high - low for _, low, high in rows)

    def body(where_ref, in_ref, *refs):
        at = 0
        for block, low, high in rows:
            shape = (high - low, step)
            along = lax.broadcasted_iota(jnp.int32, shape, 0) + (where_ref[0] + low)
            across = lax.broadcasted_iota(jnp.int32, shape, 1) + (where_ref[1] + pl.program_id(0) * step)
            refs[-1][at : at + high - low] = jnp.where(
                across >= along + block * where_ref[2], in_ref[block, low:high], 0.0
            )
            at += high - low

    return pl.pallas_call(
        body,
        grid=(here // step,),
        in_specs=[SCALARS, pl.BlockSpec((2, share, step), lambda i: (0, 0, i))]
        + [pl.BlockSpec(memory_space=pl.ANY)] * len(after),
        out_specs=pl.BlockSpec((height, step), lambda i: (0, i)),
        out_shape=jax.ShapeDtypeStruct((height, here), F32),
        compiler_params=params(8),
        cost_estimate=cost(0, 4 * vectors.size * 2),
        name=name,
    )(where, vectors, *after)


def project(name, rows, partners, eigvecs, bit=None):
    here, nc = eigvecs.shape
    step = min(here, 512)
    height = sum(count for _, count, _ in rows)
    extra = sum(count for _, count, _ in partners)
    steps = here // step

    def body(*refs):
        refs = list(refs)
        bit_ref = refs.pop(0) if bit is not None else None
        row_refs, partner_refs = refs[: len(rows)], refs[len(rows) : len(rows) + len(partners)]
        eig_ref = refs[len(rows) + len(partners)]
        outs, acc = refs[len(rows) + len(partners) + 1 : -1], refs[-1]
        k = pl.program_id(0)

        @pl.when(k == 0)
        def _():
            acc[...] = jnp.zeros_like(acc)

        vh, vl = split(jnp.concatenate([r[...] for r in row_refs]))
        acc[:, :nc] += three(vh, vl, eig_ref[...], NN)
        if partners:
            acc[:, nc:] += three(vh, vl, jnp.concatenate([r[...] for r in partner_refs]), NT)

        @pl.when(k == steps - 1)
        def _():
            if bit is None:
                outs[0][...] = acc[...]
            else:
                half = height // 2
                zero = bit_ref[0] == 0
                outs[0][...] = jnp.where(zero, acc[:half], acc[half:])
                outs[1][...] = jnp.where(zero, acc[half:], acc[:half])

    outputs = 1 if bit is None else 2
    shape = (height // outputs, nc + extra)
    return pl.pallas_call(
        body,
        grid=(steps,),
        in_specs=([] if bit is None else [SCALARS])
        + strips(rows + partners, step)
        + [pl.BlockSpec((step, nc), lambda i: (i, 0))],
        out_specs=[whole(shape)] * outputs,
        out_shape=[jax.ShapeDtypeStruct(shape, F32)] * outputs,
        scratch_shapes=[pltpu.VMEM((height, nc + extra), F32)],
        compiler_params=params(ROOM),
        cost_estimate=cost(6 * height * here * (nc + extra), 4 * (eigvecs.size + height * here)),
        name=name,
    )(*([] if bit is None else [bit]), *[r[0] for r in rows + partners], eigvecs)


def turn(name, pieces):
    here = pieces[0][0].shape[1]
    step = min(here, 512)
    height = sum(count for _, count, _ in pieces)

    def body(*refs):
        turned = jnp.concatenate([r[...] for r in refs[:-2]]).T
        high, low = split(turned)
        refs[-2][...] = high
        refs[-1][...] = low

    return pl.pallas_call(
        body,
        grid=(here // step,),
        in_specs=strips(pieces, step),
        out_specs=[pl.BlockSpec((step, height), lambda i: (i, 0))] * 2,
        out_shape=[jax.ShapeDtypeStruct((here, height), BF16)] * 2,
        compiler_params=params(ROOM),
        cost_estimate=cost(0, 8 * height * here),
        name=name,
    )(*[r[0] for r in pieces])


def reorder(where, factors, share, chips, segments):
    width = factors.shape[1]

    def body(where_ref, in_ref, *outs):
        chip, core = where_ref[3], where_ref[4]
        for block, out in enumerate(outs):
            picks = []
            for step, other, low, high in segments[block]:
                at = (lax.rem(chip + step, chips) * 2 + (core + other) % 2) * share + low
                shape = (high - low, width)
                same = lax.broadcasted_iota(jnp.int32, shape, 1) == lax.broadcasted_iota(jnp.int32, shape, 0) + at
                picks.append(jnp.where(same, 1.0, 0.0))
            pick = jnp.concatenate(picks)
            out[...] = full_dot(full_dot(pick, in_ref[block]), pick, NT)

    return pl.pallas_call(
        body,
        grid=(1,),
        in_specs=[SCALARS, whole(factors.shape)],
        out_specs=[whole((width, width))] * 2,
        out_shape=[jax.ShapeDtypeStruct((width, width), F32)] * 2,
        compiler_params=params(ROOM),
        cost_estimate=cost(48 * width**3, 8 * factors.size),
        name="reorder",
    )(where, factors)


def update(name, make, ins, factor, turned, current, with_scaled):
    here, nc = current.shape
    width = factor.shape[0]
    step = min(here, 512)

    def body(*refs):
        in_refs, rest = refs[: len(ins)], refs[len(ins) :]
        factor_ref, high_ref, low_ref, cur_ref = rest[:4]
        outs, (sh_ref, sl_ref) = rest[4:-2], rest[-2:]

        @pl.when(pl.program_id(0) == 0)
        def _():
            scaled = full_dot(factor_ref[...], make(*in_refs))
            sh_ref[...], sl_ref[...] = split(scaled)
            if with_scaled:
                outs[1][...] = scaled

        high, low = high_ref[...], low_ref[...]
        sh, sl = sh_ref[...], sl_ref[...]
        dot = functools.partial(jnp.dot, preferred_element_type=F32)
        outs[0][...] = cur_ref[...] - (dot(high, sh) + dot(high, sl) + dot(low, sh))

    def spec(value):
        return SCALARS if value.dtype == jnp.int32 else whole(value.shape)

    tall = pl.BlockSpec((step, width), lambda i: (i, 0))
    wide = pl.BlockSpec((step, nc), lambda i: (i, 0))
    out_specs, out_shape = [wide], [jax.ShapeDtypeStruct((here, nc), F32)]
    if with_scaled:
        out_specs.append(whole((width, nc)))
        out_shape.append(jax.ShapeDtypeStruct((width, nc), F32))
    return pl.pallas_call(
        body,
        grid=(here // step,),
        in_specs=[spec(v) for v in ins] + [whole(factor.shape), tall, tall, wide],
        out_specs=out_specs,
        out_shape=out_shape,
        scratch_shapes=[pltpu.VMEM((width, nc), BF16)] * 2,
        compiler_params=params(ROOM),
        cost_estimate=cost(6 * here * width * nc, 4 * here * (2 * nc + width)),
        name=name,
    )(*ins, factor, *turned, current)


def make_local(chips, rows):
    cols = 2 * chips

    def core_swap(value):
        return lax.ppermute(value, "col", [(i, i ^ 1) for i in range(cols)])

    def from_chip(value, step):
        return lax.ppermute(value, "col", [((i + 2 * step) % cols, i) for i in range(cols)])

    def row_swap(value, step):
        return lax.ppermute(value, "row", [(i, i ^ step) for i in range(rows)])

    def sums(value, send=None):
        step = 1
        if send is not None:
            got = row_swap(send, 1)
            yield got
            value, step = value + got, 2
        while step < rows:
            got = row_swap(value, step)
            yield got
            value, step = value + got, 2 * step
        if send is not None:
            other = row_swap(value, 1)
            yield other
            value = (value, other)
        return value

    def local(vectors, factors, eigvecs):
        share, here = vectors.shape[1:]
        nc = eigvecs.shape[1]
        width = share * cols
        half = 2 * share
        col, row = lax.axis_index("col"), lax.axis_index("row")
        where = jnp.stack([col * share, row * here, jnp.int32(width), col // 2, col % 2]).astype(jnp.int32)
        bit = (row % 2).astype(jnp.int32)[None]
        pieces = []
        for block, low, high in PIECES:
            low, high = low * share // 64 // 8 * 8, high * share // 64 // 8 * 8
            pieces.append((block, low, high))

        def after(value, *others):
            return lax.optimization_barrier((value, *others))[0]

        far, last = [], ()
        for n, (block, low, high) in enumerate(pieces):
            sent = cut(where, vectors, last, [(block, low, high)], f"cut_{n}")
            far += [(step, (block, low, high), from_chip(sent, step)) for step in range(1, chips)]
            last = (sent,)
        mine = cut(where, vectors, last, [(1, 0, share), (0, 0, share)], "cut_own")
        sib = core_swap(mine)
        own = {1: [(mine, share, 0), (sib, share, 0)], 0: [(mine, share, 1), (sib, share, 1)]}
        segments = {k: [(0, 0, 0, share), (0, 1, 0, share)] for k in (0, 1)}
        all_ones, all_zeros = list(own[1]), list(own[0])
        running, done, waits = [], {}, ()

        def advance():
            got = []
            for key, chain in list(running):
                try:
                    got.append(next(chain))
                except StopIteration as end:
                    done[key] = end.value
                    running.remove((key, chain))
            return got

        first = project("project_own", own[1] + own[0], own[0], eigvecs, bit)
        running.append(("own", sums(*first)))
        front = first
        for n, (step, (block, low, high), value) in enumerate(far):
            value = after(value, *front, *waits)
            waits = advance()
            pair = [(v, high - low, 0) for v in (value, core_swap(value))]
            segments[block] += [(step, 0, low, high), (step, 1, low, high)]
            if block == 1:
                all_ones += pair
                front = project(f"project_one_{n}", pair, own[0], eigvecs, bit)
            else:
                all_zeros += pair
                front = project(f"project_zero_{n}", pair, all_ones, eigvecs)
            running.append((n, sums(*front)))
        while running:
            advance()
        ones = [done["own"]] + [done[n] for n, f in enumerate(far) if f[1][0] == 1]
        zeros = [done[n] for n, f in enumerate(far) if f[1][0] == 0]
        t0, t1 = reorder(where, factors, share, chips, segments)

        flat = [v for pair in ones for v in pair]

        def joined(bit_ref, refs, columns):
            parts = []
            zero = bit_ref[0] == 0
            for a, b in zip(refs[::2], refs[1::2]):
                a, b = a[:, columns], b[:, columns]
                parts.append((jnp.where(zero, a, b), jnp.where(zero, b, a)))
            ones = [parts[0][0]] + [p for pair in parts[1:] for p in pair]
            return jnp.concatenate(ones), parts[0][1]

        def make_one(bit_ref, *refs):
            return joined(bit_ref, refs, slice(0, nc))[0]

        def make_zero(bit_ref, scaled_ref, *refs):
            ones_refs, zero_refs = refs[: len(flat)], refs[len(flat) :]
            scaled = scaled_ref[...]
            turned_gram = joined(bit_ref, ones_refs, slice(nc, nc + half))[0]
            parts = [joined(bit_ref, ones_refs[:2], slice(0, nc))[1] - full_dot(turned_gram, scaled, TN)]
            later = jnp.concatenate([r[...] for r in zero_refs])
            parts.append(later[:, :nc] - full_dot(later[:, nc:], scaled))
            return jnp.concatenate(parts)

        current, scaled = update("update_one", make_one, [bit, *flat], t1, turn("turn_one", all_ones), eigvecs, True)
        (out,) = update("update_zero", make_zero, [bit, scaled, *flat, *zeros], t0, turn("turn_zero", all_zeros), current, False)
        return out

    return local


def solution(mesh):
    placed = (P("groups", "col", "row"), P("groups", None, None), P(("groups", "row"), "col"))
    local = make_local(mesh.shape["col"] // 2, mesh.shape["row"])
    return jax.shard_map(
        local, mesh=mesh, in_specs=placed, out_specs=P(("groups", "row"), "col"), check_vma=False
    )
```

```python
import jax
import jax.numpy as jnp
from jax import lax
from jax.experimental import pallas as pl
from jax.experimental.pallas import tpu as pltpu
from jax.sharding import PartitionSpec as P

F32, BF16 = jnp.float32, jnp.bfloat16
PIECES = ((1, 0, 32), (1, 32, 64), (0, 0, 40), (0, 40, 64))
SWAP_PARTS = 2
NN = (((1,), (0,)), ((), ()))
NT = (((1,), (1,)), ((), ()))
TN = (((0,), (0,)), ((), ()))
SCALARS = pl.BlockSpec(memory_space=pltpu.SMEM)
VMEM = pl.BlockSpec(memory_space=pltpu.VMEM)
HBM = pl.BlockSpec(memory_space=pltpu.HBM)
ANY = pl.BlockSpec(memory_space=pl.ANY)


def call(body, name, ins, specs, outs, out_specs, scratch=(), mib=16):
    return pl.pallas_call(
        body,
        in_specs=specs,
        out_specs=out_specs,
        out_shape=outs,
        scratch_shapes=list(scratch),
        compiler_params=pltpu.CompilerParams(vmem_limit_bytes=mib * 1024 * 1024),
        cost_estimate=pl.CostEstimate(flops=1, bytes_accessed=1, transcendentals=0),
        name=name,
    )(*ins)


def array(*shape, dtype=F32):
    return jax.ShapeDtypeStruct(shape, dtype)


def split(value):
    high = value.astype(BF16)
    return high, (value - high.astype(F32)).astype(BF16)


def dot(a, b, dims=NN):
    return lax.dot_general(a, b, dims, preferred_element_type=F32)


def full_dot(a, b, dims=NN):
    return lax.dot_general(a, b, dims, precision=lax.Precision.HIGHEST, preferred_element_type=F32)


def three(vh, vl, bh, bl, dims):
    rows = vh.shape[0]
    first = dot(jnp.concatenate([vh, vl]), bh, dims)
    return first[:rows] + first[rows:] + dot(vh, bl, dims)


def steps_of(here, step):
    step = min(here, step)
    return [pl.ds(at, step) for at in range(0, here, step)]


def cut(name, where, vectors, after, rows):
    here = vectors.shape[2]
    places, height = [], 0
    for block, low, high in rows:
        places.append((block, low, high, height))
        height += high - low

    def body(where_ref, in_ref, *refs):
        out, sems = refs[-2:]
        copies = [
            pltpu.make_async_copy(in_ref.at[block, low:high], out.at[at : at + high - low], sems.at[n])
            for n, (block, low, high, at) in enumerate(places)
        ]
        for copy in copies:
            copy.start()
        for copy, (block, low, high, at) in zip(copies, places):
            copy.wait()
            shape = (high - low, here)
            along = lax.broadcasted_iota(jnp.int32, shape, 0) + (where_ref[0] + low + block * where_ref[2])
            across = lax.broadcasted_iota(jnp.int32, shape, 1) + where_ref[1]
            out[at : at + high - low] = jnp.where(across >= along, out[at : at + high - low], 0.0)

    return call(
        body,
        name,
        (where, vectors, *after),
        [SCALARS, HBM] + [ANY] * len(after),
        array(height, here),
        VMEM,
        [pltpu.SemaphoreType.DMA((len(rows),))],
    )


def load(eigvecs):
    here, nc = eigvecs.shape
    steps = steps_of(here, 512)

    def body(in_ref, out, high, low, sems):
        copies = [pltpu.make_async_copy(in_ref.at[ds], out.at[ds], sems.at[n]) for n, ds in enumerate(steps)]
        for copy in copies:
            copy.start()
        for copy, ds in zip(copies, steps):
            copy.wait()
            high[ds, :], low[ds, :] = split(out[ds, :])

    outs = [array(here, nc), array(here, nc, dtype=BF16), array(here, nc, dtype=BF16)]
    sems = [pltpu.SemaphoreType.DMA((len(steps),))]
    return call(body, "load", (eigvecs,), [HBM], outs, [VMEM] * 3, sems)


def rows_of(refs, pieces, ds):
    return jnp.concatenate([ref[at : at + count, ds] for ref, (_, count, at) in zip(refs, pieces)])


def project(name, rows, partners, high, low, bit=None):
    here, nc = high.shape
    height = sum(count for _, count, _ in rows)
    extra = sum(count for _, count, _ in partners)
    steps = steps_of(here, 512)

    def body(*refs):
        refs = list(refs)
        acc = refs.pop()
        bit_ref = refs.pop(0) if bit is not None else None
        row_refs, refs = refs[: len(rows)], refs[len(rows) :]
        partner_refs, refs = refs[: len(partners)], refs[len(partners) :]
        high_ref, low_ref = refs[:2]
        outs = refs[2:]
        for n, ds in enumerate(steps):
            vh, vl = split(rows_of(row_refs, rows, ds))
            main = three(vh, vl, high_ref[ds, :], low_ref[ds, :], NN)
            gram = three(vh, vl, *split(rows_of(partner_refs, partners, ds)), NT)
            if n == 0:
                acc[:, :nc], acc[:, nc:] = main, gram
            else:
                acc[:, :nc] += main
                acc[:, nc:] += gram
        if bit is None:
            outs[0][...] = acc[...]
        else:
            half = height // 2
            zero = bit_ref[0] == 0
            outs[0][...] = jnp.where(zero, acc[:half], acc[half:])
            outs[1][...] = jnp.where(zero, acc[half:], acc[:half])

    outputs = 1 if bit is None else 2
    arrays = [r[0] for r in rows + partners] + [high, low]
    return call(
        body,
        name,
        ([] if bit is None else [bit]) + arrays,
        ([] if bit is None else [SCALARS]) + [VMEM] * len(arrays),
        [array(height // outputs, nc + extra)] * outputs,
        [VMEM] * outputs,
        [pltpu.VMEM((height, nc + extra), F32)],
    )


def reorder(where, factors, after, share, chips, segments):
    width = factors.shape[1]

    def body(where_ref, in_ref, *refs):
        chip, core = where_ref[3], where_ref[4]
        for block, out in enumerate(refs[-2:]):
            picks = []
            for step, other, low, high in segments[block]:
                at = (lax.rem(chip + step, chips) * 2 + (core + other) % 2) * share + low
                shape = (high - low, width)
                same = lax.broadcasted_iota(jnp.int32, shape, 1) == lax.broadcasted_iota(jnp.int32, shape, 0) + at
                picks.append(jnp.where(same, 1.0, 0.0))
            pick = jnp.concatenate(picks)
            out[...] = full_dot(full_dot(pick, in_ref[block]), pick, NT)

    specs = [SCALARS, VMEM] + [ANY] * len(after)
    return call(body, "reorder", (where, factors, *after), specs, [array(width, width)] * 2, [VMEM] * 2)


def update(name, make, ins, factor, pieces, current, last):
    here, nc = current.shape
    width = factor.shape[0]
    steps = steps_of(here, 256)

    def body(*refs):
        in_refs, refs = refs[: len(ins)], refs[len(ins) :]
        factor_ref, refs = refs[0], refs[1:]
        piece_refs, refs = refs[: len(pieces)], refs[len(pieces) :]
        cur_ref, out = refs[:2]
        scaled = full_dot(factor_ref[...], make(*in_refs))
        sh, sl = split(scaled)
        if not last:
            refs[2][...] = scaled
        copies = []
        for n, ds in enumerate(steps):
            vh, vl = split(rows_of(piece_refs, pieces, ds))
            new = cur_ref[ds, :] - (dot(vh, sh, TN) + dot(vh, sl, TN) + dot(vl, sh, TN))
            if last:
                held, sems = refs[2:]
                held[ds, :] = new
                copies.append(pltpu.make_async_copy(held.at[ds], out.at[ds], sems.at[n]))
                copies[-1].start()
            else:
                out[ds, :] = new
        for copy in copies:
            copy.wait()

    specs = [SCALARS if v.dtype == jnp.int32 else VMEM for v in ins] + [VMEM] * (len(pieces) + 2)
    args = [*ins, factor, *[p[0] for p in pieces], current]
    if last:
        scratch = [pltpu.VMEM((here, nc), F32), pltpu.SemaphoreType.DMA((len(steps),))]
        return call(body, name, args, specs, array(here, nc), HBM, scratch, 24)
    return call(body, name, args, specs, [array(here, nc), array(width, nc)], [VMEM] * 2)


def make_local(chips, rows):
    cols = 2 * chips

    def core_swap(value):
        return lax.ppermute(value, "col", [(i, i ^ 1) for i in range(cols)])

    def from_chip(value, step):
        return lax.ppermute(value, "col", [((i + 2 * step) % cols, i) for i in range(cols)])

    def row_swap(value, step):
        return lax.ppermute(value, "row", [(i, i ^ step) for i in range(rows)])

    def sums(value, send=None):
        step, got = 1, None
        if send is not None:
            got = row_swap(send, 1)
            yield got
            step = 2
        while step < rows:
            value = value if got is None else value + got
            got = row_swap(value, step)
            yield got
            step *= 2
        if send is not None:
            value = value + got
            got = row_swap(value, 1)
            yield got
        return value, got

    def local(vectors, factors, eigvecs):
        share, here = vectors.shape[1:]
        nc = eigvecs.shape[1]
        width = share * cols
        half = 2 * share
        col, row = lax.axis_index("col"), lax.axis_index("row")
        where = jnp.stack([col * share, row * here, jnp.int32(width), col // 2, col % 2]).astype(jnp.int32)
        bit = (row % 2).astype(jnp.int32)[None]
        pieces = []
        for block, low, high in PIECES:
            low, high = low * share // 64 // 8 * 8, high * share // 64 // 8 * 8
            pieces.append((block, low, high))

        def after(value, *others):
            return lax.optimization_barrier((value, *others))[0]

        far, last = [], ()
        for n, piece in enumerate(pieces):
            sent = cut(f"cut_{n}", where, vectors, last, [piece])
            far += [(step, piece, from_chip(sent, step)) for step in range(1, chips)]
            if n == 0:
                mine = cut("cut_own", where, vectors, (sent,), [(1, 0, share), (0, 0, share)])
                sib = core_swap(mine)
                current, high, low = load(after(eigvecs, mine))
                last = (high,)
        own = {1: [(mine, share, 0), (sib, share, 0)], 0: [(mine, share, share), (sib, share, share)]}
        segments = {k: [(0, 0, 0, share), (0, 1, 0, share)] for k in (0, 1)}
        all_ones, all_zeros = list(own[1]), list(own[0])
        running, done, waits = [], {}, ()

        def advance():
            got = []
            for key, chain in list(running):
                try:
                    got.append(next(chain))
                except StopIteration as end:
                    done[key] = end.value
                    running.remove((key, chain))
            return got

        front = project("project_own", own[1] + own[0], own[0], high, low, bit)
        running.append(("own", sums(*front)))
        for n, (step, (block, first, final), value) in enumerate(far):
            value = after(value, *front, *waits)
            waits = advance()
            pair = [(value, final - first, 0)]
            parts = SWAP_PARTS if (final - first) % (8 * SWAP_PARTS) == 0 else 1
            each = (final - first) // parts
            for part in range(parts):
                pair.append((core_swap(value[part * each : (part + 1) * each]), each, 0))
            segments[block] += [(step, 0, first, final), (step, 1, first, final)]
            if block == 1:
                all_ones += pair
                front = project(f"project_one_{n}", pair, own[0], high, low, bit)
            else:
                all_zeros += pair
                front = project(f"project_zero_{n}", pair, all_ones, high, low)
            running.append((n, sums(*front)))
        while running:
            advance()
        ones = [done["own"]] + [done[n] for n, f in enumerate(far) if f[1][0] == 1]
        zeros = [v for n, f in enumerate(far) if f[1][0] == 0 for v in done[n]]
        t0, t1 = reorder(where, factors, front, share, chips, segments)
        flat = [v for pair in ones for v in pair]

        def joined(bit_ref, refs, columns):
            parts = []
            zero = bit_ref[0] == 0
            for a, b in zip(refs[::2], refs[1::2]):
                a, b = a[:, columns], b[:, columns]
                parts.append((jnp.where(zero, a, b), jnp.where(zero, b, a)))
            ones = [parts[0][0]] + [p for pair in parts[1:] for p in pair]
            return jnp.concatenate(ones), parts[0][1]

        def make_one(bit_ref, *refs):
            return joined(bit_ref, refs, slice(0, nc))[0]

        def make_zero(bit_ref, scaled_ref, *refs):
            ones_refs, zero_refs = refs[: len(flat)], refs[len(flat) :]
            scaled = scaled_ref[...]
            turned_gram = joined(bit_ref, ones_refs, slice(nc, nc + half))[0]
            parts = [joined(bit_ref, ones_refs[:2], slice(0, nc))[1] - full_dot(turned_gram, scaled, TN)]
            later = jnp.concatenate([a[...] + b[...] for a, b in zip(zero_refs[::2], zero_refs[1::2])])
            parts.append(later[:, :nc] - full_dot(later[:, nc:], scaled))
            return jnp.concatenate(parts)

        current, scaled = update("update_one", make_one, [bit, *flat], t1, all_ones, current, False)
        return update("update_zero", make_zero, [bit, scaled, *flat, *zeros], t0, all_zeros, current, True)

    return local


def solution(mesh):
    placed = (P("groups", "col", "row"), P("groups", None, None), P(("groups", "row"), "col"))
    local = make_local(mesh.shape["col"] // 2, mesh.shape["row"])
    return jax.shard_map(
        local, mesh=mesh, in_specs=placed, out_specs=P(("groups", "row"), "col"), check_vma=False
    )
```

```python
import jax
import jax.numpy as jnp
from jax import lax
from jax.experimental import pallas as pl
from jax.experimental.pallas import tpu as pltpu
from jax.sharding import PartitionSpec as P

F32, BF16 = jnp.float32, jnp.bfloat16
PIECES = ((1, 0, 32, True), (1, 32, 64, True), (0, 0, 48, True), (0, 48, 64, False))
SWAP_PARTS = 2
NN = (((1,), (0,)), ((), ()))
NT = (((1,), (1,)), ((), ()))
TN = (((0,), (0,)), ((), ()))
SCALARS = pl.BlockSpec(memory_space=pltpu.SMEM)
VMEM = pl.BlockSpec(memory_space=pltpu.VMEM)
HBM = pl.BlockSpec(memory_space=pltpu.HBM)


def call(body, name, ins, specs, outs, out_specs, scratch=(), mib=8):
    return pl.pallas_call(
        body,
        in_specs=specs,
        out_specs=out_specs,
        out_shape=outs,
        scratch_shapes=list(scratch),
        compiler_params=pltpu.CompilerParams(vmem_limit_bytes=mib * 1024 * 1024),
        cost_estimate=pl.CostEstimate(flops=1, bytes_accessed=1, transcendentals=0),
        name=name,
    )(*ins)


def array(*shape, dtype=F32):
    return jax.ShapeDtypeStruct(shape, dtype)


def split(value):
    high = value.astype(BF16)
    return high, (value - high.astype(F32)).astype(BF16)


def dot(a, b, dims=NN):
    return lax.dot_general(a, b, dims, preferred_element_type=F32)


def full_dot(a, b, dims=NN):
    return lax.dot_general(a, b, dims, precision=lax.Precision.HIGHEST, preferred_element_type=F32)


def three(vh, vl, bh, bl, dims):
    rows = vh.shape[0]
    first = dot(jnp.concatenate([vh, vl]), bh, dims)
    return first[:rows] + first[rows:] + dot(vh, bl, dims)


def steps_of(here, step):
    step = min(here, step)
    return [pl.ds(at, step) for at in range(0, here, step)]


def cut(where, vectors, first):
    _, share, here = vectors.shape
    block, low, high = first
    begin = (1 - block) * share + low

    def body(where_ref, in_ref, piece, mine, sems):
        copies = [
            pltpu.make_async_copy(in_ref.at[k], mine.at[(1 - k) * share : (2 - k) * share], sems.at[k]) for k in (0, 1)
        ]
        copies[1].start()
        copies[0].start()
        for k in (1, 0):
            copies[k].wait()
            shape = (share, here)
            along = lax.broadcasted_iota(jnp.int32, shape, 0) + (where_ref[0] + k * where_ref[2])
            across = lax.broadcasted_iota(jnp.int32, shape, 1) + where_ref[1]
            rows = slice((1 - k) * share, (2 - k) * share)
            mine[rows] = jnp.where(across >= along, mine[rows], 0.0)
        piece[...] = mine[begin : begin + high - low]

    outs = [array(high - low, here), array(2 * share, here)]
    return call(body, "cut", (where, vectors), [SCALARS, HBM], outs, [VMEM] * 2, [pltpu.SemaphoreType.DMA((2,))], 56)


def parts_of(mine, places):
    here = mine.shape[1]

    def body(in_ref, *refs):
        for (low, high), out in zip(places, refs):
            out[...] = in_ref[low:high]

    outs = [array(high - low, here) for low, high in places]
    return call(body, "parts", (mine,), [VMEM], outs, [VMEM] * len(outs), mib=2)


def load(eigvecs):
    here, nc = eigvecs.shape
    steps = steps_of(here, 512)

    def body(in_ref, high, low, held, sems):
        copies = [pltpu.make_async_copy(in_ref.at[ds], held.at[ds], sems.at[n]) for n, ds in enumerate(steps)]
        for copy in copies:
            copy.start()
        for copy, ds in zip(copies, steps):
            copy.wait()
            high[ds, :], low[ds, :] = split(held[ds, :])

    scratch = [pltpu.VMEM((here, nc), F32), pltpu.SemaphoreType.DMA((len(steps),))]
    return call(body, "load", (eigvecs,), [HBM], [array(here, nc, dtype=BF16)] * 2, [VMEM] * 2, scratch, 44)


def rows_of(refs, pieces, ds):
    return jnp.concatenate([ref[at : at + count, ds] for ref, (_, count, at) in zip(refs, pieces)])


def project(name, rows, partners, high, low, bit=None, gram_rows=None):
    here, nc = high.shape
    height = sum(count for _, count, _ in rows)
    extra = sum(count for _, count, _ in partners)
    some = height if gram_rows is None else gram_rows
    steps = steps_of(here, 512)

    def body(*refs):
        refs = list(refs)
        acc = refs.pop()
        bit_ref = refs.pop(0) if bit is not None else None
        row_refs, refs = refs[: len(rows)], refs[len(rows) :]
        partner_refs, refs = refs[: len(partners)], refs[len(partners) :]
        high_ref, low_ref = refs[:2]
        outs = refs[2:]
        for n, ds in enumerate(steps):
            vh, vl = split(rows_of(row_refs, rows, ds))
            main = three(vh, vl, high_ref[ds, :], low_ref[ds, :], NN)
            gram = three(vh[:some], vl[:some], *split(rows_of(partner_refs, partners, ds)), NT)
            if n == 0:
                acc[:, :nc], acc[:some, nc:] = main, gram
                if some < height:
                    acc[some:, nc:] = jnp.zeros((height - some, extra), F32)
            else:
                acc[:, :nc] += main
                acc[:some, nc:] += gram
        if bit is None:
            outs[0][...] = acc[...]
        else:
            half = height // 2
            zero = bit_ref[5] == 0
            outs[0][...] = jnp.where(zero, acc[:half], acc[half:])
            outs[1][...] = jnp.where(zero, acc[half:], acc[:half])

    outputs = 1 if bit is None else 2
    arrays = [r[0] for r in rows + partners] + [high, low]
    return call(
        body,
        name,
        ([] if bit is None else [bit]) + arrays,
        ([] if bit is None else [SCALARS]) + [VMEM] * len(arrays),
        [array(height // outputs, nc + extra)] * outputs,
        [VMEM] * outputs,
        [pltpu.VMEM((height, nc + extra), F32)],
    )


def reorder(where, factors, share, chips, segments):
    width = factors.shape[1]

    def body(where_ref, in_ref, *outs):
        chip, core = where_ref[3], where_ref[4]
        for block, out in enumerate(outs):
            picks = []
            for step, other, low, high in segments[block]:
                at = (lax.rem(chip + step, chips) * 2 + (core + other) % 2) * share + low
                shape = (high - low, width)
                same = lax.broadcasted_iota(jnp.int32, shape, 1) == lax.broadcasted_iota(jnp.int32, shape, 0) + at
                picks.append(jnp.where(same, 1.0, 0.0))
            pick = jnp.concatenate(picks)
            out[...] = full_dot(full_dot(pick, in_ref[block]), pick, NT)

    return call(body, "reorder", (where, factors), [SCALARS, VMEM], [array(width, width)] * 2, [VMEM] * 2)


def update(name, make, ins, factor, pieces, current, last):
    here, nc = current.shape
    width = factor.shape[0]
    steps = steps_of(here, 256)

    def body(*refs):
        in_refs, refs = refs[: len(ins)], refs[len(ins) :]
        factor_ref, refs = refs[0], refs[1:]
        piece_refs, refs = refs[: len(pieces)], refs[len(pieces) :]
        cur_ref, out = refs[:2]
        loads = []
        if not last:
            held, sems = refs[3:]
            loads = [pltpu.make_async_copy(cur_ref.at[ds], held.at[ds], sems.at[n]) for n, ds in enumerate(steps)]
            for copy in loads:
                copy.start()
            cur_ref = held
        scaled = full_dot(factor_ref[...], make(*in_refs))
        sh, sl = split(scaled)
        if not last:
            refs[2][...] = scaled
        copies = []
        for n, ds in enumerate(steps):
            vh, vl = split(rows_of(piece_refs, pieces, ds))
            if loads:
                loads[n].wait()
            new = cur_ref[ds, :] - (dot(vh, sh, TN) + dot(vh, sl, TN) + dot(vl, sh, TN))
            if last:
                held, sems = refs[2:]
                held[ds, :] = new
                copies.append(pltpu.make_async_copy(held.at[ds], out.at[ds], sems.at[n]))
                copies[-1].start()
            else:
                out[ds, :] = new
        for copy in copies:
            copy.wait()

    specs = [SCALARS if v.dtype == jnp.int32 else VMEM for v in ins] + [VMEM] * (len(pieces) + 1)
    specs.append(VMEM if last else HBM)
    args = [*ins, factor, *[p[0] for p in pieces], current]
    scratch = [pltpu.VMEM((here, nc), F32), pltpu.SemaphoreType.DMA((len(steps),))]
    if last:
        return call(body, name, args, specs, array(here, nc), HBM, scratch, 13)
    return call(body, name, args, specs, [array(here, nc), array(width, nc)], [VMEM] * 2, scratch, 13)


def make_local(chips, rows):
    cols = 2 * chips

    def core_swap(value):
        return lax.ppermute(value, "col", [(i, i ^ 1) for i in range(cols)])

    def from_chip(value, step):
        return lax.ppermute(value, "col", [((i + 2 * step) % cols, i) for i in range(cols)])

    def row_swap(value, step):
        return lax.ppermute(value, "row", [(i, i ^ step) for i in range(rows)])

    def sums(value, send=None):
        step, got = 1, None
        if send is not None:
            got = row_swap(send, 1)
            yield got
            step = 2
        while step < rows:
            value = value if got is None else value + got
            got = row_swap(value, step)
            yield got
            step *= 2
        if send is not None:
            value = value + got
            got = row_swap(value, 1)
            yield got
        return value, got

    def local(vectors, factors, eigvecs):
        share, here = vectors.shape[1:]
        nc = eigvecs.shape[1]
        width = share * cols
        half = 2 * share
        col, row = lax.axis_index("col"), lax.axis_index("row")
        where = jnp.stack([col * share, row * here, jnp.int32(width), col // 2, col % 2, row % 2]).astype(jnp.int32)
        bit = where
        pieces = []
        for block, low, high, _ in PIECES:
            low, high = low * share // 64 // 8 * 8, high * share // 64 // 8 * 8
            pieces.append((block, low, high))
        halves = {piece: chosen for piece, (*_, chosen) in zip(pieces, PIECES)}

        def after(value, *others):
            return lax.optimization_barrier((value, *others))[0]

        sent, mine = cut(where, vectors, pieces[0])
        far = [(step, pieces[0], from_chip(sent, step)) for step in range(1, chips)]
        sib = core_swap(mine)
        high, low = load(after(eigvecs, mine))
        places = [((1 - block) * share + a, (1 - block) * share + b) for block, a, b in pieces[1:]]
        for piece, sent in zip(pieces[1:], parts_of(after(mine, high), places)):
            far += [(step, piece, from_chip(sent, step)) for step in range(1, chips)]
        own = {1: [(mine, share, 0), (sib, share, 0)], 0: [(mine, share, share), (sib, share, share)]}
        segments = {k: [(0, 0, 0, share), (0, 1, 0, share)] for k in (0, 1)}
        all_ones, all_zeros = list(own[1]), list(own[0])
        running, done, waits = [], {}, ()

        def advance():
            got = []
            for key, chain in list(running):
                try:
                    got.append(next(chain))
                except StopIteration as end:
                    done[key] = end.value
                    running.remove((key, chain))
            return got

        front = project("project_own", own[1] + own[0], own[0], high, low, bit, half)
        running.append(("own", sums(*front)))
        for n, (step, (block, first, final), value) in enumerate(far):
            value = after(value, *front, *waits)
            waits = advance()
            split_rows = halves[block, first, final]
            pair = [(value, final - first, 0)]
            parts = SWAP_PARTS if (final - first) % (8 * SWAP_PARTS) == 0 else 1
            each = (final - first) // parts
            for part in range(parts):
                pair.append((core_swap(value[part * each : (part + 1) * each]), each, 0))
            segments[block] += [(step, 0, first, final), (step, 1, first, final)]
            if block == 1:
                all_ones += pair
                front = project(f"project_one_{n}", pair, own[0], high, low, bit if split_rows else None)
            else:
                all_zeros += pair
                front = project(f"project_zero_{n}", pair, all_ones, high, low, bit if split_rows else None)
            running.append((n, sums(*front)))
        while running:
            advance()
        ones = [("own", True)] + [(n, halves[f[1]]) for n, f in enumerate(far) if f[1][0] == 1]
        zeros = [(n, halves[f[1]]) for n, f in enumerate(far) if f[1][0] == 0]
        t0, t1 = reorder(where, after(factors, *front), share, chips, segments)
        ones_flat, zeros_flat = ([v for key, _ in group for v in done[key]] for group in (ones, zeros))

        def joined(where_ref, refs, group, columns):
            parts = []
            zero = where_ref[5] == 0
            for a, b, (_, chosen) in zip(refs[::2], refs[1::2], group):
                a, b = a[:, columns], b[:, columns]
                parts += [jnp.where(zero, a, b), jnp.where(zero, b, a)] if chosen else [a + b]
            return parts

        def make_one(where_ref, *refs):
            parts = joined(where_ref, refs, ones, slice(0, nc))
            return jnp.concatenate(parts[:1] + parts[2:])

        def make_zero(where_ref, scaled_ref, *refs):
            ones_refs, zero_refs = refs[: len(ones_flat)], refs[len(ones_flat) :]
            scaled = scaled_ref[...]
            parts = joined(where_ref, ones_refs, ones, slice(nc, nc + half))
            turned_gram = jnp.concatenate(parts[:1] + parts[2:])
            front = joined(where_ref, ones_refs[:2], ones[:1], slice(0, nc))[1] - full_dot(turned_gram, scaled, TN)
            later = jnp.concatenate(joined(where_ref, zero_refs, zeros, slice(None)))
            return jnp.concatenate([front, later[:, :nc] - full_dot(later[:, nc:], scaled)])

        current, scaled = update("update_one", make_one, [bit, *ones_flat], t1, all_ones, eigvecs, False)
        ins = [bit, scaled, *ones_flat, *zeros_flat]
        return update("update_zero", make_zero, ins, t0, all_zeros, current, True)

    return local


def solution(mesh):
    placed = (P("groups", "col", "row"), P("groups", None, None), P(("groups", "row"), "col"))
    local = make_local(mesh.shape["col"] // 2, mesh.shape["row"])
    return jax.shard_map(
        local, mesh=mesh, in_specs=placed, out_specs=P(("groups", "row"), "col"), check_vma=False
    )
```

```python
import jax
import jax.numpy as jnp
from jax import lax
from jax.experimental import pallas as pl
from jax.experimental.pallas import tpu as pltpu
from jax.sharding import PartitionSpec as P

F32, BF16 = jnp.float32, jnp.bfloat16
PIECES = ((1, 0, 64, True), (0, 0, 48, True), (0, 48, 64, False))
SWAP_PARTS = 2
NN = (((1,), (0,)), ((), ()))
NT = (((1,), (1,)), ((), ()))
TN = (((0,), (0,)), ((), ()))
SCALARS = pl.BlockSpec(memory_space=pltpu.SMEM)
VMEM = pl.BlockSpec(memory_space=pltpu.VMEM)
HBM = pl.BlockSpec(memory_space=pltpu.HBM)


def call(body, name, ins, specs, outs, out_specs, scratch=(), mib=8):
    return pl.pallas_call(
        body,
        in_specs=specs,
        out_specs=out_specs,
        out_shape=outs,
        scratch_shapes=list(scratch),
        compiler_params=pltpu.CompilerParams(vmem_limit_bytes=mib * 1024 * 1024),
        cost_estimate=pl.CostEstimate(flops=1, bytes_accessed=1, transcendentals=0),
        name=name,
    )(*ins)


def array(*shape, dtype=F32):
    return jax.ShapeDtypeStruct(shape, dtype)


def split(value):
    high = value.astype(BF16)
    return high, (value - high.astype(F32)).astype(BF16)


def dot(a, b, dims=NN):
    return lax.dot_general(a, b, dims, preferred_element_type=F32)


def full_dot(a, b, dims=NN):
    return lax.dot_general(a, b, dims, precision=lax.Precision.HIGHEST, preferred_element_type=F32)


def three(vh, vl, bh, bl, dims):
    rows = vh.shape[0]
    first = dot(jnp.concatenate([vh, vl]), bh, dims)
    return first[:rows] + first[rows:] + dot(vh, bl, dims)


def short_dot(a, b, dims=NN):
    (ah, al), (bh, bl) = split(a), split(b)
    return dot(ah, bh, dims) + dot(ah, bl, dims) + dot(al, bh, dims)


def steps_of(here, step):
    step = min(here, step)
    return [pl.ds(at, step) for at in range(0, here, step)]


def cut(where, vectors, first):
    _, share, here = vectors.shape
    block, low, high = first
    begin = (1 - block) * share + low

    strip = min(share, 16)
    strips = [(k, at) for k in (1, 0) for at in range(0, share, strip)]

    def body(where_ref, in_ref, piece, mine, sems):
        copies = []
        for n, (k, at) in enumerate(strips):
            to = mine.at[(1 - k) * share + at : (1 - k) * share + at + strip]
            copies.append(pltpu.make_async_copy(in_ref.at[k, at : at + strip], to, sems.at[n]))
            copies[-1].start()
        for copy, (k, at) in zip(copies, strips):
            copy.wait()
            shape = (strip, here)
            along = lax.broadcasted_iota(jnp.int32, shape, 0) + (where_ref[0] + at + k * where_ref[2])
            across = lax.broadcasted_iota(jnp.int32, shape, 1) + where_ref[1]
            rows = slice((1 - k) * share + at, (1 - k) * share + at + strip)
            mine[rows] = jnp.where(across >= along, mine[rows], 0.0)
        piece[...] = mine[begin : begin + high - low]

    outs = [array(high - low, here), array(2 * share, here)]
    sems = [pltpu.SemaphoreType.DMA((len(strips),))]
    return call(body, "cut", (where, vectors), [SCALARS, HBM], outs, [VMEM] * 2, sems, 56)


def parts_of(mine, places):
    here = mine.shape[1]

    def body(in_ref, *refs):
        for (low, high), out in zip(places, refs):
            out[...] = in_ref[low:high]

    outs = [array(high - low, here) for low, high in places]
    return call(body, "parts", (mine,), [VMEM], outs, [VMEM] * len(outs), mib=2)


def load(eigvecs):
    here, nc = eigvecs.shape
    steps = steps_of(here, 512)

    def body(in_ref, high, low, held, sems):
        copies = [pltpu.make_async_copy(in_ref.at[ds], held.at[ds], sems.at[n]) for n, ds in enumerate(steps)]
        for copy in copies:
            copy.start()
        for copy, ds in zip(copies, steps):
            copy.wait()
            high[ds, :], low[ds, :] = split(held[ds, :])

    scratch = [pltpu.VMEM((here, nc), F32), pltpu.SemaphoreType.DMA((len(steps),))]
    return call(body, "load", (eigvecs,), [HBM], [array(here, nc, dtype=BF16)] * 2, [VMEM] * 2, scratch, 44)


def rows_of(refs, pieces, ds):
    return jnp.concatenate([ref[at : at + count, ds] for ref, (_, count, at) in zip(refs, pieces)])


def project(name, rows, partners, high, low, bit=None, gram_rows=None):
    here, nc = high.shape
    height = sum(count for _, count, _ in rows)
    extra = sum(count for _, count, _ in partners)
    some = height if gram_rows is None else gram_rows
    steps = steps_of(here, 512)

    def body(*refs):
        refs = list(refs)
        acc = refs.pop()
        bit_ref = refs.pop(0) if bit is not None else None
        row_refs, refs = refs[: len(rows)], refs[len(rows) :]
        partner_refs, refs = refs[: len(partners)], refs[len(partners) :]
        high_ref, low_ref = refs[:2]
        outs = refs[2:]
        for n, ds in enumerate(steps):
            vh, vl = split(rows_of(row_refs, rows, ds))
            main = three(vh, vl, high_ref[ds, :], low_ref[ds, :], NN)
            gram = three(vh[:some], vl[:some], *split(rows_of(partner_refs, partners, ds)), NT)
            if n == 0:
                acc[:, :nc], acc[:some, nc:] = main, gram
                if some < height:
                    acc[some:, nc:] = jnp.zeros((height - some, extra), F32)
            else:
                acc[:, :nc] += main
                acc[:some, nc:] += gram
        if bit is None:
            outs[0][...] = acc[...]
        else:
            half = height // 2
            zero = bit_ref[5] == 0
            outs[0][...] = jnp.where(zero, acc[:half], acc[half:])
            outs[1][...] = jnp.where(zero, acc[half:], acc[:half])

    outputs = 1 if bit is None else 2
    arrays = [r[0] for r in rows + partners] + [high, low]
    return call(
        body,
        name,
        ([] if bit is None else [bit]) + arrays,
        ([] if bit is None else [SCALARS]) + [VMEM] * len(arrays),
        [array(height // outputs, nc + extra)] * outputs,
        [VMEM] * outputs,
        [pltpu.VMEM((height, nc + extra), F32)],
    )


def reorder(where, factors, share, chips, segments):
    width = factors.shape[1]

    def body(where_ref, in_ref, *outs):
        chip, core = where_ref[3], where_ref[4]
        for block, out in enumerate(outs):
            picks = []
            for step, other, low, high in segments[block]:
                at = (lax.rem(chip + step, chips) * 2 + (core + other) % 2) * share + low
                shape = (high - low, width)
                same = lax.broadcasted_iota(jnp.int32, shape, 1) == lax.broadcasted_iota(jnp.int32, shape, 0) + at
                picks.append(jnp.where(same, 1.0, 0.0))
            pick = jnp.concatenate(picks)
            out[...] = full_dot(full_dot(pick, in_ref[block]), pick, NT)

    return call(body, "reorder", (where, factors), [SCALARS, VMEM], [array(width, width)] * 2, [VMEM] * 2)


def update(name, make, ins, factor, pieces, current, last):
    here, nc = current[0].shape
    width = factor.shape[0]
    steps = steps_of(here, 256)

    def body(*refs):
        in_refs, refs = refs[: len(ins)], refs[len(ins) :]
        factor_ref, refs = refs[0], refs[1:]
        piece_refs, refs = refs[: len(pieces)], refs[len(pieces) :]
        cur_refs, refs = refs[: len(current)], refs[len(current) :]
        out = refs[0]
        scaled = short_dot(factor_ref[...], make(*in_refs))
        sh, sl = split(scaled)
        if not last:
            refs[1][...] = scaled
        copies = []
        for n, ds in enumerate(steps):
            vh, vl = split(rows_of(piece_refs, pieces, ds))
            new = cur_refs[0][ds, :].astype(F32)
            for ref in cur_refs[1:]:
                new += ref[ds, :].astype(F32)
            new -= dot(vh, sh, TN) + dot(vh, sl, TN) + dot(vl, sh, TN)
            if last:
                held, sems = refs[1:]
                held[ds, :] = new
                copies.append(pltpu.make_async_copy(held.at[ds], out.at[ds], sems.at[n]))
                copies[-1].start()
            else:
                out[ds, :] = new
        for copy in copies:
            copy.wait()

    args = [*ins, factor, *[p[0] for p in pieces], *current]
    specs = [SCALARS if v.dtype == jnp.int32 else VMEM for v in args]
    if last:
        scratch = [pltpu.VMEM((here, nc), F32), pltpu.SemaphoreType.DMA((len(steps),))]
        return call(body, name, args, specs, array(here, nc), HBM, scratch, 13)
    return call(body, name, args, specs, [array(here, nc), array(width, nc)], [VMEM] * 2)


def make_local(chips, rows):
    cols = 2 * chips

    def core_swap(value):
        return lax.ppermute(value, "col", [(i, i ^ 1) for i in range(cols)])

    def from_chip(value, step):
        return lax.ppermute(value, "col", [((i + 2 * step) % cols, i) for i in range(cols)])

    def row_swap(value, step):
        return lax.ppermute(value, "row", [(i, i ^ step) for i in range(rows)])

    def sums(value, send=None):
        step, got = 1, None
        if send is not None:
            got = yield row_swap(send, 1)
            step = 2
        while step < rows:
            value = value if got is None else value + got
            got = yield row_swap(value, step)
            step *= 2
        if send is not None:
            value = value + got
            got = yield row_swap(value, 1)
        return value, got

    def local(vectors, factors, eigvecs):
        share, here = vectors.shape[1:]
        nc = eigvecs.shape[1]
        width = share * cols
        half = 2 * share
        col, row = lax.axis_index("col"), lax.axis_index("row")
        where = jnp.stack([col * share, row * here, jnp.int32(width), col // 2, col % 2, row % 2]).astype(jnp.int32)
        bit = where
        pieces = []
        for block, low, high, _ in PIECES:
            low, high = low * share // 64 // 8 * 8, high * share // 64 // 8 * 8
            pieces.append((block, low, high))
        halves = {piece: chosen for piece, (*_, chosen) in zip(pieces, PIECES)}

        def after(value, *others):
            return lax.optimization_barrier((value, *others))[0]

        sent, mine = cut(where, vectors, pieces[0])
        far = [(step, pieces[0], from_chip(sent, step)) for step in range(1, chips)]
        sib = core_swap(mine)
        high, low = load(after(eigvecs, mine))
        places = [((1 - block) * share + a, (1 - block) * share + b) for block, a, b in pieces[1:]]
        for piece, sent in zip(pieces[1:], parts_of(after(mine, high), places)):
            far += [(step, piece, from_chip(sent, step)) for step in range(1, chips)]
        own = {1: [(mine, share, 0), (sib, share, 0)], 0: [(mine, share, share), (sib, share, share)]}
        segments = {k: [(0, 0, 0, share), (0, 1, 0, share)] for k in (0, 1)}
        all_ones, all_zeros = list(own[1]), list(own[0])
        running, flying, done = {}, {}, {}

        def start(*names):
            for name in names:
                if name not in running:
                    continue
                try:
                    flying[name] = running[name].send(flying.pop(name, None))
                except StopIteration as end:
                    done[name] = end.value
                    del running[name]

        def arrived(*names):
            return [flying[name] for name in names if name in flying]

        front = project("project_own", own[1] + own[0], own[0], high, low, bit, half)
        running["own"] = sums(*front)
        start("own")
        last = len(far) - 1
        for n, (step, (block, first, final), value) in enumerate(far):
            waits = list(running) if n < last or last != 2 else []
            value = after(value, *front, *arrived(*waits))
            start(*waits)
            split_rows = halves[block, first, final]
            pair = [(value, final - first, 0)]
            parts = SWAP_PARTS if (final - first) % (8 * SWAP_PARTS) == 0 else 1
            each = (final - first) // parts
            for part in range(parts):
                pair.append((core_swap(value[part * each : (part + 1) * each]), each, 0))
            segments[block] += [(step, 0, first, final), (step, 1, first, final)]
            ready = high
            if n == last == 2:
                ready = after(high, *arrived(0, 1))
                start(0, 1)
            if block == 1:
                all_ones += pair
                front = project(f"project_one_{n}", pair, own[0], ready, low, bit if split_rows else None)
            else:
                all_zeros += pair
                front = project(f"project_zero_{n}", pair, all_ones, ready, low, bit if split_rows else None)
            running[n] = sums(*front)
            start(n)
        if last in flying:
            flying[last] = after(flying[last], *arrived("own", 0))
        while running:
            start(*list(running))
        ones = [("own", True)] + [(n, halves[f[1]]) for n, f in enumerate(far) if f[1][0] == 1]
        zeros = [(n, halves[f[1]]) for n, f in enumerate(far) if f[1][0] == 0]
        t0, t1 = reorder(where, after(factors, *front), share, chips, segments)
        ones_flat, zeros_flat = ([v for key, _ in group for v in done[key]] for group in (ones, zeros))

        def joined(where_ref, refs, group, columns):
            parts = []
            zero = where_ref[5] == 0
            for a, b, (_, chosen) in zip(refs[::2], refs[1::2], group):
                a, b = a[:, columns], b[:, columns]
                parts += [jnp.where(zero, a, b), jnp.where(zero, b, a)] if chosen else [a + b]
            return parts

        def make_one(where_ref, *refs):
            parts = joined(where_ref, refs, ones, slice(0, nc))
            return jnp.concatenate(parts[:1] + parts[2:])

        def make_zero(where_ref, scaled_ref, *refs):
            ones_refs, zero_refs = refs[: len(ones_flat)], refs[len(ones_flat) :]
            scaled = scaled_ref[...]
            parts = joined(where_ref, ones_refs, ones, slice(nc, nc + half))
            turned_gram = jnp.concatenate(parts[:1] + parts[2:])
            front = joined(where_ref, ones_refs[:2], ones[:1], slice(0, nc))[1] - short_dot(turned_gram, scaled, TN)
            later = jnp.concatenate(joined(where_ref, zero_refs, zeros, slice(None)))
            return jnp.concatenate([front, later[:, :nc] - short_dot(later[:, nc:], scaled)])

        current, scaled = update("update_one", make_one, [bit, *ones_flat], t1, all_ones, [high, low], False)
        ins = [bit, scaled, *ones_flat, *zeros_flat]
        return update("update_zero", make_zero, ins, t0, all_zeros, [current], True)

    return local


def solution(mesh):
    placed = (P("groups", "col", "row"), P("groups", None, None), P(("groups", "row"), "col"))
    local = make_local(mesh.shape["col"] // 2, mesh.shape["row"])
    return jax.shard_map(
        local, mesh=mesh, in_specs=placed, out_specs=P(("groups", "row"), "col"), check_vma=False
    )
```

```python
import jax
import jax.numpy as jnp
from jax import lax
from jax.experimental import pallas as pl
from jax.experimental.pallas import tpu as pltpu
from jax.sharding import PartitionSpec as P

F32, BF16 = jnp.float32, jnp.bfloat16
PIECES = ((1, 0, 64, True), (0, 0, 40, True), (0, 40, 64, False))
SWAP_ROWS = (16, 16, 32)
NN = (((1,), (0,)), ((), ()))
NT = (((1,), (1,)), ((), ()))
TN = (((0,), (0,)), ((), ()))
SCALARS = pl.BlockSpec(memory_space=pltpu.SMEM)
VMEM = pl.BlockSpec(memory_space=pltpu.VMEM)
HBM = pl.BlockSpec(memory_space=pltpu.HBM)


def call(body, name, ins, specs, outs, out_specs, scratch=(), mib=8):
    return pl.pallas_call(
        body,
        in_specs=specs,
        out_specs=out_specs,
        out_shape=outs,
        scratch_shapes=list(scratch),
        compiler_params=pltpu.CompilerParams(vmem_limit_bytes=mib * 1024 * 1024),
        cost_estimate=pl.CostEstimate(flops=1, bytes_accessed=1, transcendentals=0),
        name=name,
    )(*ins)


def array(*shape, dtype=F32):
    return jax.ShapeDtypeStruct(shape, dtype)


def split(value):
    high = value.astype(BF16)
    return high, (value - high.astype(F32)).astype(BF16)


def dot(a, b, dims=NN):
    return lax.dot_general(a, b, dims, preferred_element_type=F32)


def full_dot(a, b, dims=NN):
    return lax.dot_general(a, b, dims, precision=lax.Precision.HIGHEST, preferred_element_type=F32)


def three(vh, vl, bh, bl, dims):
    rows = vh.shape[0]
    first = dot(jnp.concatenate([vh, vl]), bh, dims)
    return first[:rows] + first[rows:] + dot(vh, bl, dims)


def short_dot(a, b, dims=NN):
    (ah, al), (bh, bl) = split(a), split(b)
    return dot(ah, bh, dims) + dot(ah, bl, dims) + dot(al, bh, dims)


def steps_of(here, step):
    step = min(here, step)
    return [pl.ds(at, step) for at in range(0, here, step)]


def cut(where, vectors, width):
    _, share, here = vectors.shape
    strip = min(share, 16)
    strips = [(k, at) for k in (1, 0) for at in range(0, share, strip)]

    def body(where_ref, in_ref, zeros, ones, sems):
        outs = (zeros, ones)
        copies = []
        for n, (k, at) in enumerate(strips):
            ds = pl.ds(at, strip)
            copies.append(pltpu.make_async_copy(in_ref.at[k, ds], outs[k].at[ds], sems.at[n]))
            copies[-1].start()
        for copy, (k, at) in zip(copies, strips):
            copy.wait()
            shape = (strip, min(here, (k + 1) * width))
            along = lax.broadcasted_iota(jnp.int32, shape, 0) + (where_ref[0] + at + k * where_ref[2])
            across = lax.broadcasted_iota(jnp.int32, shape, 1) + where_ref[1]
            part = outs[k][at : at + strip, : shape[1]]
            outs[k][at : at + strip, : shape[1]] = jnp.where(across >= along, part, 0.0)

    sems = [pltpu.SemaphoreType.DMA((len(strips),))]
    return call(body, "cut", (where, vectors), [SCALARS, HBM], [array(share, here)] * 2, [VMEM] * 2, sems, 4)


def parts_of(mine, places):
    here = mine.shape[1]

    def body(in_ref, *refs):
        for (low, high), out in zip(places, refs):
            out[...] = in_ref[low:high]

    outs = [array(high - low, here) for low, high in places]
    return call(body, "parts", (mine,), [VMEM], outs, [VMEM] * len(outs), mib=2)


def load(eigvecs):
    here, nc = eigvecs.shape
    steps = steps_of(here, 512)

    def body(in_ref, high, low, held, sems):
        copies = [pltpu.make_async_copy(in_ref.at[ds], held.at[ds], sems.at[n]) for n, ds in enumerate(steps)]
        for copy in copies:
            copy.start()
        for copy, ds in zip(copies, steps):
            copy.wait()
            high[ds, :], low[ds, :] = split(held[ds, :])

    scratch = [pltpu.VMEM((here, nc), F32), pltpu.SemaphoreType.DMA((len(steps),))]
    return call(body, "load", (eigvecs,), [HBM], [array(here, nc, dtype=BF16)] * 2, [VMEM] * 2, scratch, 44)


def rows_of(refs, pieces, ds):
    return jnp.concatenate([ref[at : at + count, ds] for ref, (_, count, at) in zip(refs, pieces)])


def project(name, rows, partners, high, low, bit=None):
    here, nc = high.shape
    height = sum(count for _, count, _ in rows)
    extra = sum(count for _, count, _ in partners)
    steps = steps_of(here, 512)

    def body(*refs):
        refs = list(refs)
        acc = refs.pop()
        bit_ref = refs.pop(0) if bit is not None else None
        row_refs, refs = refs[: len(rows)], refs[len(rows) :]
        partner_refs, refs = refs[: len(partners)], refs[len(partners) :]
        high_ref, low_ref = refs[:2]
        outs = refs[2:]
        for n, ds in enumerate(steps):
            vh, vl = split(rows_of(row_refs, rows, ds))
            main = three(vh, vl, high_ref[ds, :], low_ref[ds, :], NN)
            if partners:
                gram = three(vh, vl, *split(rows_of(partner_refs, partners, ds)), NT)
                main = jnp.concatenate([main, gram], axis=1)
            if n == 0:
                acc[...] = main
            else:
                acc[...] += main
        if bit is None:
            outs[0][...] = acc[...]
        else:
            half = height // 2
            zero = bit_ref[5] == 0
            outs[0][...] = jnp.where(zero, acc[:half], acc[half:])
            outs[1][...] = jnp.where(zero, acc[half:], acc[:half])

    outputs = 1 if bit is None else 2
    arrays = [r[0] for r in rows + partners] + [high, low]
    return call(
        body,
        name,
        ([] if bit is None else [bit]) + arrays,
        ([] if bit is None else [SCALARS]) + [VMEM] * len(arrays),
        [array(height // outputs, nc + extra)] * outputs,
        [VMEM] * outputs,
        [pltpu.VMEM((height, nc + extra), F32)],
    )


def reorder(where, factors, share, chips, segments):
    width = factors.shape[1]

    def body(where_ref, in_ref, *outs):
        chip, core = where_ref[3], where_ref[4]
        for block, out in enumerate(outs):
            picks = []
            for step, other, low, high in segments[block]:
                at = (lax.rem(chip + step, chips) * 2 + (core + other) % 2) * share + low
                shape = (high - low, width)
                same = lax.broadcasted_iota(jnp.int32, shape, 1) == lax.broadcasted_iota(jnp.int32, shape, 0) + at
                picks.append(jnp.where(same, 1.0, 0.0))
            pick = jnp.concatenate(picks)
            out[...] = full_dot(full_dot(pick, in_ref[block]), pick, NT)

    return call(body, "reorder", (where, factors), [SCALARS, VMEM], [array(width, width)] * 2, [VMEM] * 2)


def update(name, make, ins, factor, pieces, current, last):
    here, nc = current[0].shape
    width = factor.shape[0]
    steps = steps_of(here, 256)

    def body(*refs):
        in_refs, refs = refs[: len(ins)], refs[len(ins) :]
        factor_ref, refs = refs[0], refs[1:]
        piece_refs, refs = refs[: len(pieces)], refs[len(pieces) :]
        cur_refs, refs = refs[: len(current)], refs[len(current) :]
        out = refs[0]
        scaled = short_dot(factor_ref[...], make(*in_refs))
        sh, sl = split(scaled)
        if not last:
            refs[1][...] = scaled
        copies = []
        for n, ds in enumerate(steps):
            vh, vl = split(rows_of(piece_refs, pieces, ds))
            new = cur_refs[0][ds, :].astype(F32)
            for ref in cur_refs[1:]:
                new += ref[ds, :].astype(F32)
            new -= dot(vh, sh, TN) + dot(vh, sl, TN) + dot(vl, sh, TN)
            if last:
                held, sems = refs[1:]
                held[ds, :] = new
                copies.append(pltpu.make_async_copy(held.at[ds], out.at[ds], sems.at[n]))
                copies[-1].start()
            else:
                out[ds, :] = new
        for copy in copies:
            copy.wait()

    args = [*ins, factor, *[p[0] for p in pieces], *current]
    specs = [SCALARS if v.dtype == jnp.int32 else VMEM for v in args]
    if last:
        scratch = [pltpu.VMEM((here, nc), F32), pltpu.SemaphoreType.DMA((len(steps),))]
        return call(body, name, args, specs, array(here, nc), HBM, scratch, 13)
    return call(body, name, args, specs, [array(here, nc), array(width, nc)], [VMEM] * 2)


def make_local(chips, rows):
    cols = 2 * chips

    def core_swap(value):
        return lax.ppermute(value, "col", [(i, i ^ 1) for i in range(cols)])

    def from_chip(value, step):
        return lax.ppermute(value, "col", [((i + 2 * step) % cols, i) for i in range(cols)])

    def row_swap(value, step):
        return lax.ppermute(value, "row", [(i, i ^ step) for i in range(rows)])

    def sums(value, send=None):
        step, got = 1, None
        if send is not None:
            got = yield row_swap(send, 1)
            step = 2
        while step < rows:
            value = value if got is None else value + got
            got = yield row_swap(value, step)
            step *= 2
        if send is not None:
            value = value + got
            got = yield row_swap(value, 1)
        return value, got

    def local(vectors, factors, eigvecs):
        share, here = vectors.shape[1:]
        nc = eigvecs.shape[1]
        width = share * cols
        half = 2 * share
        col, row = lax.axis_index("col"), lax.axis_index("row")
        where = jnp.stack([col * share, row * here, jnp.int32(width), col // 2, col % 2, row % 2]).astype(jnp.int32)
        bit = where
        pieces = []
        for block, low, high, _ in PIECES:
            low, high = low * share // 64 // 8 * 8, high * share // 64 // 8 * 8
            pieces.append((block, low, high))
        swap_rows = dict(zip(pieces, SWAP_ROWS))
        halves = {piece: chosen for piece, (*_, chosen) in zip(pieces, PIECES)}

        def after(value, *others):
            return lax.optimization_barrier((value, *others))[0]

        mine = cut(where, vectors, width)
        whole = [(step, pieces[0], from_chip(mine[1], step)) for step in range(1, chips)]
        sib = [core_swap(m) for m in mine]
        high, low = load(after(eigvecs, *mine))
        far, places = whole, [(a, b) for _, a, b in pieces[1:]]
        for piece, sent in zip(pieces[1:], parts_of(after(mine[0], high), places)):
            far += [(step, piece, from_chip(sent, step)) for step in range(1, chips)]
        own = {k: [(mine[k], share, 0), (sib[k], share, 0)] for k in (0, 1)}
        segments = {k: [(0, 0, 0, share), (0, 1, 0, share)] for k in (0, 1)}
        for step, (block, a, b), _ in far:
            segments[block] += [(step, 0, a, b), (step, 1, a, b)]
        all_ones, all_zeros = list(own[1]), list(own[0])
        running, flying, done = {}, {}, {}

        def start(*names):
            for name in names:
                if name not in running:
                    continue
                try:
                    flying[name] = running[name].send(flying.pop(name, None))
                except StopIteration as end:
                    done[name] = end.value
                    del running[name]

        def arrived(*names):
            return [flying[name] for name in names if name in flying]

        keep, send = project("project_own1", own[1], own[0], high, low, bit)
        running["own1"] = sums(keep, send)
        start("own1")
        front = project("project_own0", own[0], [], after(high, keep), low, bit)
        running["own0"] = sums(*front)
        start("own0")
        t0, t1 = reorder(where, after(factors, *front), share, chips, segments)
        front = (*front, t0)
        last = len(far) - 1
        for n, (step, (block, first, final), value) in enumerate(far):
            waits = list(running) if last != 2 else (("own1", "own0"), ("own1", 0, "own0"), ("own1",))[n]
            value = after(value, *front, *arrived(*waits))
            start(*waits if last != 2 else (("own1", "own0"), ("own1",), ())[n])
            split_rows = halves[block, first, final]
            pair = [(value, final - first, 0)]
            for at in range(0, final - first, swap_rows[block, first, final]):
                upto = min(at + swap_rows[block, first, final], final - first)
                pair.append((core_swap(value[at:upto]), upto - at, 0))
            if block == 1:
                all_ones += pair
                front = project(f"project_one_{n}", pair, own[0], high, low, bit if split_rows else None)
            else:
                all_zeros += pair
                front = project(f"project_zero_{n}", pair, all_ones, high, low, bit if split_rows else None)
            running[n] = sums(*front)
            start(n)
            if n == 1 and last == 2:
                flying[0] = after(flying[0], *front)
                start(0)
        if last == 2:
            flying["own0"] = after(flying["own0"], *front)
            flying[last] = after(flying[last], *arrived(0))
            start("own0", 0)
        while running:
            start(*list(running))
        ones = [("own1", True)] + [(n, halves[f[1]]) for n, f in enumerate(far) if f[1][0] == 1]
        zeros = [("own0", True)] + [(n, halves[f[1]]) for n, f in enumerate(far) if f[1][0] == 0]
        ones_flat, zeros_flat = ([v for key, _ in group for v in done[key]] for group in (ones, zeros))

        def joined(where_ref, refs, group, columns):
            parts = []
            zero = where_ref[5] == 0
            for a, b, (_, chosen) in zip(refs[::2], refs[1::2], group):
                a, b = a[:, columns], b[:, columns]
                parts += [jnp.where(zero, a, b), jnp.where(zero, b, a)] if chosen else [a + b]
            return parts

        def make_one(where_ref, *refs):
            return jnp.concatenate(joined(where_ref, refs, ones, slice(0, nc)))

        def make_zero(where_ref, scaled_ref, *refs):
            ones_refs, zero_refs = refs[: len(ones_flat)], refs[len(ones_flat) :]
            scaled = scaled_ref[...]
            turned_gram = jnp.concatenate(joined(where_ref, ones_refs, ones, slice(nc, nc + half)))
            front = jnp.concatenate(joined(where_ref, zero_refs[:2], zeros[:1], slice(None)))
            later = jnp.concatenate(joined(where_ref, zero_refs[2:], zeros[1:], slice(None)))
            front -= short_dot(turned_gram, scaled, TN)
            return jnp.concatenate([front, later[:, :nc] - short_dot(later[:, nc:], scaled)])

        current, scaled = update("update_one", make_one, [bit, *ones_flat], t1, all_ones, [high, low], False)
        ins = [bit, scaled, *ones_flat, *zeros_flat]
        return update("update_zero", make_zero, ins, t0, all_zeros, [current], True)

    return local


def solution(mesh):
    placed = (P("groups", "col", "row"), P("groups", None, None), P(("groups", "row"), "col"))
    local = make_local(mesh.shape["col"] // 2, mesh.shape["row"])
    return jax.shard_map(
        local, mesh=mesh, in_specs=placed, out_specs=P(("groups", "row"), "col"), check_vma=False
    )
```

```python
import jax
import jax.numpy as jnp
from jax import lax
from jax.experimental import pallas as pl
from jax.experimental.pallas import tpu as pltpu
from jax.sharding import PartitionSpec as P

F32, BF16 = jnp.float32, jnp.bfloat16
PIECES = ((1, 0, 64, True), (0, 0, 40, True), (0, 40, 64, False))
SWAP_ROWS = (16, 16, 8)
NN = (((1,), (0,)), ((), ()))
NT = (((1,), (1,)), ((), ()))
TN = (((0,), (0,)), ((), ()))
SCALARS = pl.BlockSpec(memory_space=pltpu.SMEM)
VMEM = pl.BlockSpec(memory_space=pltpu.VMEM)
HBM = pl.BlockSpec(memory_space=pltpu.HBM)


def call(body, name, ins, specs, outs, out_specs, scratch=(), mib=8):
    return pl.pallas_call(
        body,
        in_specs=specs,
        out_specs=out_specs,
        out_shape=outs,
        scratch_shapes=list(scratch),
        compiler_params=pltpu.CompilerParams(vmem_limit_bytes=mib * 1024 * 1024),
        cost_estimate=pl.CostEstimate(flops=1, bytes_accessed=1, transcendentals=0),
        name=name,
    )(*ins)


def array(*shape, dtype=F32):
    return jax.ShapeDtypeStruct(shape, dtype)


def split(value):
    high = value.astype(BF16)
    return high, (value - high.astype(F32)).astype(BF16)


def dot(a, b, dims=NN):
    return lax.dot_general(a, b, dims, preferred_element_type=F32)


def full_dot(a, b, dims=NN):
    return lax.dot_general(a, b, dims, precision=lax.Precision.HIGHEST, preferred_element_type=F32)


def three(vh, vl, bh, bl, dims):
    rows = vh.shape[0]
    first = dot(jnp.concatenate([vh, vl]), bh, dims)
    return first[:rows] + first[rows:] + dot(vh, bl, dims)


def short_dot(a, b, dims=NN):
    (ah, al), (bh, bl) = split(a), split(b)
    return dot(ah, bh, dims) + dot(ah, bl, dims) + dot(al, bh, dims)


def steps_of(here, step):
    step = min(here, step)
    return [pl.ds(at, step) for at in range(0, here, step)]


def cut(where, vectors, width):
    _, share, here = vectors.shape
    strip = min(share, 16)
    strips = [(k, at) for k in (1, 0) for at in range(0, share, strip)]

    def body(where_ref, in_ref, zeros, ones, sems):
        outs = (zeros, ones)
        copies = []
        for n, (k, at) in enumerate(strips):
            ds = pl.ds(at, strip)
            copies.append(pltpu.make_async_copy(in_ref.at[k, ds], outs[k].at[ds], sems.at[n]))
            copies[-1].start()
        for copy, (k, at) in zip(copies, strips):
            copy.wait()
            shape = (strip, min(here, (k + 1) * width))
            along = lax.broadcasted_iota(jnp.int32, shape, 0) + (where_ref[0] + at + k * where_ref[2])
            across = lax.broadcasted_iota(jnp.int32, shape, 1) + where_ref[1]
            part = outs[k][at : at + strip, : shape[1]]
            outs[k][at : at + strip, : shape[1]] = jnp.where(across >= along, part, 0.0)

    sems = [pltpu.SemaphoreType.DMA((len(strips),))]
    return call(body, "cut", (where, vectors), [SCALARS, HBM], [array(share, here)] * 2, [VMEM] * 2, sems, 4)


def parts_of(mine, places):
    here = mine.shape[1]

    def body(in_ref, *refs):
        for (low, high), out in zip(places, refs):
            out[...] = in_ref[low:high]

    outs = [array(high - low, here) for low, high in places]
    return call(body, "parts", (mine,), [VMEM], outs, [VMEM] * len(outs), mib=2)


def load(eigvecs):
    here, nc = eigvecs.shape
    steps = steps_of(here, 512)

    def body(in_ref, high, low, held, sems):
        copies = [pltpu.make_async_copy(in_ref.at[ds], held.at[ds], sems.at[n]) for n, ds in enumerate(steps)]
        for copy in copies:
            copy.start()
        for copy, ds in zip(copies, steps):
            copy.wait()
            high[ds, :], low[ds, :] = split(held[ds, :])

    scratch = [pltpu.VMEM((here, nc), F32), pltpu.SemaphoreType.DMA((len(steps),))]
    return call(body, "load", (eigvecs,), [HBM], [array(here, nc, dtype=BF16)] * 2, [VMEM] * 2, scratch, 44)


def rows_of(refs, pieces, ds):
    return jnp.concatenate([ref[at : at + count, ds] for ref, (_, count, at) in zip(refs, pieces)])


def project(name, rows, partners, high, low, bit=None):
    here, nc = high.shape
    height = sum(count for _, count, _ in rows)
    extra = sum(count for _, count, _ in partners)
    steps = steps_of(here, 512)

    def body(*refs):
        refs = list(refs)
        acc = refs.pop()
        bit_ref = refs.pop(0) if bit is not None else None
        row_refs, refs = refs[: len(rows)], refs[len(rows) :]
        partner_refs, refs = refs[: len(partners)], refs[len(partners) :]
        high_ref, low_ref = refs[:2]
        outs = refs[2:]
        for n, ds in enumerate(steps):
            vh, vl = split(rows_of(row_refs, rows, ds))
            main = three(vh, vl, high_ref[ds, :], low_ref[ds, :], NN)
            if partners:
                gram = three(vh, vl, *split(rows_of(partner_refs, partners, ds)), NT)
                main = jnp.concatenate([main, gram], axis=1)
            if n == 0:
                acc[...] = main
            else:
                acc[...] += main
        if bit is None:
            outs[0][...] = acc[...]
        else:
            half = height // 2
            zero = bit_ref[5] == 0
            outs[0][...] = jnp.where(zero, acc[:half], acc[half:])
            outs[1][...] = jnp.where(zero, acc[half:], acc[:half])

    outputs = 1 if bit is None else 2
    arrays = [r[0] for r in rows + partners] + [high, low]
    return call(
        body,
        name,
        ([] if bit is None else [bit]) + arrays,
        ([] if bit is None else [SCALARS]) + [VMEM] * len(arrays),
        [array(height // outputs, nc + extra)] * outputs,
        [VMEM] * outputs,
        [pltpu.VMEM((height, nc + extra), F32)],
    )


def reorder(where, factors, share, chips, segments):
    width = factors.shape[1]

    def body(where_ref, in_ref, *outs):
        chip, core = where_ref[3], where_ref[4]
        for block, out in enumerate(outs):
            picks = []
            for step, other, low, high in segments[block]:
                at = (lax.rem(chip + step, chips) * 2 + (core + other) % 2) * share + low
                shape = (high - low, width)
                same = lax.broadcasted_iota(jnp.int32, shape, 1) == lax.broadcasted_iota(jnp.int32, shape, 0) + at
                picks.append(jnp.where(same, 1.0, 0.0))
            pick = jnp.concatenate(picks)
            out[...] = full_dot(full_dot(pick, in_ref[block]), pick, NT)

    return call(body, "reorder", (where, factors), [SCALARS, VMEM], [array(width, width)] * 2, [VMEM] * 2)


def update(name, make, ins, factor, pieces, current, last):
    here, nc = current[0].shape
    width = factor.shape[0]
    steps = steps_of(here, 256)

    def body(*refs):
        in_refs, refs = refs[: len(ins)], refs[len(ins) :]
        factor_ref, refs = refs[0], refs[1:]
        piece_refs, refs = refs[: len(pieces)], refs[len(pieces) :]
        cur_refs, refs = refs[: len(current)], refs[len(current) :]
        out = refs[0]
        scaled = short_dot(factor_ref[...], make(*in_refs))
        sh, sl = split(scaled)
        if not last:
            refs[1][...] = scaled
        copies = []
        for n, ds in enumerate(steps):
            vh, vl = split(rows_of(piece_refs, pieces, ds))
            new = cur_refs[0][ds, :].astype(F32)
            for ref in cur_refs[1:]:
                new += ref[ds, :].astype(F32)
            new -= dot(vh, sh, TN) + dot(vh, sl, TN) + dot(vl, sh, TN)
            if last:
                held, sems = refs[1:]
                held[ds, :] = new
                copies.append(pltpu.make_async_copy(held.at[ds], out.at[ds], sems.at[n]))
                copies[-1].start()
            else:
                out[ds, :] = new
        for copy in copies:
            copy.wait()

    args = [*ins, factor, *[p[0] for p in pieces], *current]
    specs = [SCALARS if v.dtype == jnp.int32 else VMEM for v in args]
    if last:
        scratch = [pltpu.VMEM((here, nc), F32), pltpu.SemaphoreType.DMA((len(steps),))]
        return call(body, name, args, specs, array(here, nc), HBM, scratch, 13)
    return call(body, name, args, specs, [array(here, nc), array(width, nc)], [VMEM] * 2)


def make_local(chips, rows):
    cols = 2 * chips

    def core_swap(value):
        return lax.ppermute(value, "col", [(i, i ^ 1) for i in range(cols)])

    def from_chip(value, step):
        return lax.ppermute(value, "col", [((i + 2 * step) % cols, i) for i in range(cols)])

    def row_swap(value, step):
        return lax.ppermute(value, "row", [(i, i ^ step) for i in range(rows)])

    def sums(value, send=None):
        step, got = 1, None
        if send is not None:
            got = yield row_swap(send, 1)
            step = 2
        while step < rows:
            value = value if got is None else value + got
            got = yield row_swap(value, step)
            step *= 2
        if send is not None:
            value = value + got
            got = yield row_swap(value, 1)
        return value, got

    def local(vectors, factors, eigvecs):
        share, here = vectors.shape[1:]
        nc = eigvecs.shape[1]
        width = share * cols
        half = 2 * share
        col, row = lax.axis_index("col"), lax.axis_index("row")
        where = jnp.stack([col * share, row * here, jnp.int32(width), col // 2, col % 2, row % 2]).astype(jnp.int32)
        bit = where
        pieces = []
        for block, low, high, _ in PIECES:
            low, high = low * share // 64 // 8 * 8, high * share // 64 // 8 * 8
            pieces.append((block, low, high))
        swap_rows = dict(zip(pieces, SWAP_ROWS))
        halves = {piece: chosen for piece, (*_, chosen) in zip(pieces, PIECES)}

        def after(value, *others):
            return lax.optimization_barrier((value, *others))[0]

        mine = cut(where, vectors, width)
        whole = [(step, pieces[0], from_chip(mine[1], step)) for step in range(1, chips)]
        sib = [core_swap(m) for m in mine]
        high, low = load(after(eigvecs, *mine))
        far, places = whole, [(a, b) for _, a, b in pieces[1:]]
        for piece, sent in zip(pieces[1:], parts_of(after(mine[0], high), places)):
            far += [(step, piece, from_chip(sent, step)) for step in range(1, chips)]
        own = {k: [(mine[k], share, 0), (sib[k], share, 0)] for k in (0, 1)}
        segments = {k: [(0, 0, 0, share), (0, 1, 0, share)] for k in (0, 1)}
        for step, (block, a, b), _ in far:
            segments[block] += [(step, 0, a, b), (step, 1, a, b)]
        all_ones, all_zeros = list(own[1]), list(own[0])
        running, flying, done = {}, {}, {}

        def start(*names):
            for name in names:
                if name not in running:
                    continue
                try:
                    flying[name] = running[name].send(flying.pop(name, None))
                except StopIteration as end:
                    done[name] = end.value
                    del running[name]

        def arrived(*names):
            return [flying[name] for name in names if name in flying]

        keep, send = project("project_own1", own[1], own[0], high, low, bit)
        running["own1"] = sums(keep, send)
        start("own1")
        front = project("project_own0", own[0], [], after(high, keep), low, bit)
        running["own0"] = sums(*front)
        start("own0")
        t0, t1 = reorder(where, after(factors, *front), share, chips, segments)
        front = (*front, t0)
        last = len(far) - 1
        for n, (step, (block, first, final), value) in enumerate(far):
            waits = list(running) if last != 2 else (("own1", "own0"), ("own1", 0, "own0"), ())[n]
            value = after(value, *front, *arrived(*waits))
            start(*waits if last != 2 else (("own1", "own0"), ("own1",), ())[n])
            split_rows = halves[block, first, final]
            pair = [(value, final - first, 0)]
            for at in range(0, final - first, swap_rows[block, first, final]):
                upto = min(at + swap_rows[block, first, final], final - first)
                pair.append((core_swap(value[at:upto]), upto - at, 0))
            ready = after(high, *arrived("own1")) if n == 2 and last == 2 else high
            if block == 1:
                all_ones += pair
                front = project(f"project_one_{n}", pair, own[0], high, low, bit if split_rows else None)
            else:
                all_zeros += pair
                front = project(f"project_zero_{n}", pair, all_ones, ready, low, bit if split_rows else None)
            running[n] = sums(*front)
            start(n)
            if n == 1 and last == 2:
                flying[0] = after(flying[0], *front)
                start(0)
        if last == 2:
            flying["own0"] = after(flying["own0"], *front)
            flying[last] = after(flying[last], *arrived(0))
            start("own0", 0)
        while running:
            start(*list(running))
        ones = [("own1", True)] + [(n, halves[f[1]]) for n, f in enumerate(far) if f[1][0] == 1]
        zeros = [("own0", True)] + [(n, halves[f[1]]) for n, f in enumerate(far) if f[1][0] == 0]
        ones_flat, zeros_flat = ([v for key, _ in group for v in done[key]] for group in (ones, zeros))

        def joined(where_ref, refs, group, columns):
            parts = []
            zero = where_ref[5] == 0
            for a, b, (_, chosen) in zip(refs[::2], refs[1::2], group):
                a, b = a[:, columns], b[:, columns]
                parts += [jnp.where(zero, a, b), jnp.where(zero, b, a)] if chosen else [a + b]
            return parts

        def make_one(where_ref, *refs):
            return jnp.concatenate(joined(where_ref, refs, ones, slice(0, nc)))

        def make_zero(where_ref, scaled_ref, *refs):
            ones_refs, zero_refs = refs[: len(ones_flat)], refs[len(ones_flat) :]
            scaled = scaled_ref[...]
            turned_gram = jnp.concatenate(joined(where_ref, ones_refs, ones, slice(nc, nc + half)))
            front = jnp.concatenate(joined(where_ref, zero_refs[:2], zeros[:1], slice(None)))
            later = jnp.concatenate(joined(where_ref, zero_refs[2:], zeros[1:], slice(None)))
            front -= short_dot(turned_gram, scaled, TN)
            return jnp.concatenate([front, later[:, :nc] - short_dot(later[:, nc:], scaled)])

        current, scaled = update("update_one", make_one, [bit, *ones_flat], t1, all_ones, [high, low], False)
        ins = [bit, scaled, *ones_flat, *zeros_flat]
        return update("update_zero", make_zero, ins, t0, all_zeros, [current], True)

    return local


def solution(mesh):
    placed = (P("groups", "col", "row"), P("groups", None, None), P(("groups", "row"), "col"))
    local = make_local(mesh.shape["col"] // 2, mesh.shape["row"])
    return jax.shard_map(
        local, mesh=mesh, in_specs=placed, out_specs=P(("groups", "row"), "col"), check_vma=False
    )
```

```python
import jax
import jax.numpy as jnp
from jax import lax
from jax.experimental import pallas as pl
from jax.experimental.pallas import tpu as pltpu
from jax.sharding import PartitionSpec as P

F32, BF16 = jnp.float32, jnp.bfloat16
PIECES = ((1, 0, 64, True), (0, 0, 40, True), (0, 40, 64, False))
SWAP_ROWS = (16, 16, 8)
NN = (((1,), (0,)), ((), ()))
NT = (((1,), (1,)), ((), ()))
TN = (((0,), (0,)), ((), ()))
SCALARS = pl.BlockSpec(memory_space=pltpu.SMEM)
VMEM = pl.BlockSpec(memory_space=pltpu.VMEM)
HBM = pl.BlockSpec(memory_space=pltpu.HBM)


def call(body, name, ins, specs, outs, out_specs, scratch=(), mib=8):
    return pl.pallas_call(
        body,
        in_specs=specs,
        out_specs=out_specs,
        out_shape=outs,
        scratch_shapes=list(scratch),
        compiler_params=pltpu.CompilerParams(vmem_limit_bytes=mib * 1024 * 1024),
        cost_estimate=pl.CostEstimate(flops=1, bytes_accessed=1, transcendentals=0),
        name=name,
    )(*ins)


def array(*shape, dtype=F32):
    return jax.ShapeDtypeStruct(shape, dtype)


def split(value):
    high = value.astype(BF16)
    return high, (value - high.astype(F32)).astype(BF16)


def dot(a, b, dims=NN):
    return lax.dot_general(a, b, dims, preferred_element_type=F32)


def full_dot(a, b, dims=NN):
    return lax.dot_general(a, b, dims, precision=lax.Precision.HIGHEST, preferred_element_type=F32)


def three(vh, vl, bh, bl, dims):
    rows = vh.shape[0]
    first = dot(jnp.concatenate([vh, vl]), bh, dims)
    return first[:rows] + first[rows:] + dot(vh, bl, dims)


def short_dot(a, b, dims=NN):
    (ah, al), (bh, bl) = split(a), split(b)
    return dot(ah, bh, dims) + dot(ah, bl, dims) + dot(al, bh, dims)


def steps_of(here, step):
    step = min(here, step)
    return [pl.ds(at, step) for at in range(0, here, step)]


def cut(where, vectors, width):
    _, share, here = vectors.shape
    strip = min(share, 16)
    strips = [(k, at) for k in (1, 0) for at in range(0, share, strip)]

    def body(where_ref, in_ref, zeros, ones, sems):
        outs = (zeros, ones)
        copies = []
        for n, (k, at) in enumerate(strips):
            ds = pl.ds(at, strip)
            copies.append(pltpu.make_async_copy(in_ref.at[k, ds], outs[k].at[ds], sems.at[n]))
            copies[-1].start()
        for copy, (k, at) in zip(copies, strips):
            copy.wait()
            shape = (strip, min(here, (k + 1) * width))
            along = lax.broadcasted_iota(jnp.int32, shape, 0) + (where_ref[0] + at + k * where_ref[2])
            across = lax.broadcasted_iota(jnp.int32, shape, 1) + where_ref[1]
            part = outs[k][at : at + strip, : shape[1]]
            outs[k][at : at + strip, : shape[1]] = jnp.where(across >= along, part, 0.0)

    sems = [pltpu.SemaphoreType.DMA((len(strips),))]
    return call(body, "cut", (where, vectors), [SCALARS, HBM], [array(share, here)] * 2, [VMEM] * 2, sems, 4)


def parts_of(mine, places):
    here = mine.shape[1]

    def body(in_ref, *refs):
        for (low, high), out in zip(places, refs):
            out[...] = in_ref[low:high]

    outs = [array(high - low, here) for low, high in places]
    return call(body, "parts", (mine,), [VMEM], outs, [VMEM] * len(outs), mib=2)


def load(eigvecs):
    here, nc = eigvecs.shape
    steps = steps_of(here, 512)

    def body(in_ref, high, low, held, sems):
        copies = [pltpu.make_async_copy(in_ref.at[ds], held.at[ds], sems.at[n]) for n, ds in enumerate(steps)]
        for copy in copies:
            copy.start()
        for copy, ds in zip(copies, steps):
            copy.wait()
            high[ds, :], low[ds, :] = split(held[ds, :])

    scratch = [pltpu.VMEM((here, nc), F32), pltpu.SemaphoreType.DMA((len(steps),))]
    return call(body, "load", (eigvecs,), [HBM], [array(here, nc, dtype=BF16)] * 2, [VMEM] * 2, scratch, 44)


def rows_of(refs, pieces, ds):
    return jnp.concatenate([ref[at : at + count, ds] for ref, (_, count, at) in zip(refs, pieces)])


def project(name, rows, partners, high, low, bit=None):
    here, nc = high.shape
    height = sum(count for _, count, _ in rows)
    extra = sum(count for _, count, _ in partners)
    steps = steps_of(here, 512)

    def body(*refs):
        refs = list(refs)
        acc = refs.pop()
        bit_ref = refs.pop(0) if bit is not None else None
        row_refs, refs = refs[: len(rows)], refs[len(rows) :]
        partner_refs, refs = refs[: len(partners)], refs[len(partners) :]
        high_ref, low_ref = refs[:2]
        outs = refs[2:]
        for n, ds in enumerate(steps):
            vh, vl = split(rows_of(row_refs, rows, ds))
            main = three(vh, vl, high_ref[ds, :], low_ref[ds, :], NN)
            if partners:
                gram = three(vh, vl, *split(rows_of(partner_refs, partners, ds)), NT)
                main = jnp.concatenate([main, gram], axis=1)
            if n == 0:
                acc[...] = main
            else:
                acc[...] += main
        if bit is None:
            outs[0][...] = acc[...]
        else:
            half = height // 2
            zero = bit_ref[5] == 0
            outs[0][...] = jnp.where(zero, acc[:half], acc[half:])
            outs[1][...] = jnp.where(zero, acc[half:], acc[:half])

    outputs = 1 if bit is None else 2
    arrays = [r[0] for r in rows + partners] + [high, low]
    return call(
        body,
        name,
        ([] if bit is None else [bit]) + arrays,
        ([] if bit is None else [SCALARS]) + [VMEM] * len(arrays),
        [array(height // outputs, nc + extra)] * outputs,
        [VMEM] * outputs,
        [pltpu.VMEM((height, nc + extra), F32)],
    )


def reorder(where, factors, share, chips, segments):
    width = factors.shape[1]

    def body(where_ref, in_ref, *outs):
        chip, core = where_ref[3], where_ref[4]
        for block, out in enumerate(outs):
            picks = []
            for step, other, low, high in segments[block]:
                at = (lax.rem(chip + step, chips) * 2 + (core + other) % 2) * share + low
                shape = (high - low, width)
                same = lax.broadcasted_iota(jnp.int32, shape, 1) == lax.broadcasted_iota(jnp.int32, shape, 0) + at
                picks.append(jnp.where(same, 1.0, 0.0))
            pick = jnp.concatenate(picks)
            out[...] = full_dot(full_dot(pick, in_ref[block]), pick, NT)

    return call(body, "reorder", (where, factors), [SCALARS, VMEM], [array(width, width)] * 2, [VMEM] * 2)


def update(name, make, ins, factor, pieces, current, last):
    here, nc = current[0].shape
    width = factor.shape[0]
    steps = steps_of(here, 512)

    def body(*refs):
        in_refs, refs = refs[: len(ins)], refs[len(ins) :]
        factor_ref, refs = refs[0], refs[1:]
        piece_refs, refs = refs[: len(pieces)], refs[len(pieces) :]
        cur_refs, refs = refs[: len(current)], refs[len(current) :]
        out = refs[0]
        scaled = short_dot(factor_ref[...], make(*in_refs))
        sh, sl = split(scaled)
        if not last:
            refs[1][...] = scaled
        copies = []
        for n, ds in enumerate(steps):
            vh, vl = split(rows_of(piece_refs, pieces, ds))
            new = cur_refs[0][ds, :].astype(F32)
            for ref in cur_refs[1:]:
                new += ref[ds, :].astype(F32)
            new -= dot(vh, sh, TN) + dot(vh, sl, TN) + dot(vl, sh, TN)
            if last:
                held, sems = refs[1:]
                held[ds, :] = new
                copies.append(pltpu.make_async_copy(held.at[ds], out.at[ds], sems.at[n]))
                copies[-1].start()
            else:
                out[ds, :] = new
        for copy in copies:
            copy.wait()

    args = [*ins, factor, *[p[0] for p in pieces], *current]
    specs = [SCALARS if v.dtype == jnp.int32 else VMEM for v in args]
    if last:
        scratch = [pltpu.VMEM((here, nc), F32), pltpu.SemaphoreType.DMA((len(steps),))]
        return call(body, name, args, specs, array(here, nc), HBM, scratch, 13)
    return call(body, name, args, specs, [array(here, nc), array(width, nc)], [VMEM] * 2)


def make_local(chips, rows):
    cols = 2 * chips

    def core_swap(value):
        return lax.ppermute(value, "col", [(i, i ^ 1) for i in range(cols)])

    def from_chip(value, step):
        return lax.ppermute(value, "col", [((i + 2 * step) % cols, i) for i in range(cols)])

    def row_swap(value, step):
        return lax.ppermute(value, "row", [(i, i ^ step) for i in range(rows)])

    def sums(value, send=None):
        step, got = 1, None
        if send is not None:
            got = yield row_swap(send, 1)
            step = 2
        while step < rows:
            value = value if got is None else value + got
            got = yield row_swap(value, step)
            step *= 2
        if send is not None:
            value = value + got
            got = yield row_swap(value, 1)
        return value, got

    def local(vectors, factors, eigvecs):
        share, here = vectors.shape[1:]
        nc = eigvecs.shape[1]
        width = share * cols
        half = 2 * share
        col, row = lax.axis_index("col"), lax.axis_index("row")
        where = jnp.stack([col * share, row * here, jnp.int32(width), col // 2, col % 2, row % 2]).astype(jnp.int32)
        bit = where
        pieces = []
        for block, low, high, _ in PIECES:
            low, high = low * share // 64 // 8 * 8, high * share // 64 // 8 * 8
            pieces.append((block, low, high))
        swap_rows = dict(zip(pieces, SWAP_ROWS))
        halves = {piece: chosen for piece, (*_, chosen) in zip(pieces, PIECES)}

        def after(value, *others):
            return lax.optimization_barrier((value, *others))[0]

        mine = cut(where, vectors, width)
        whole = [(step, pieces[0], from_chip(mine[1], step)) for step in range(1, chips)]
        sib = [core_swap(m) for m in mine]
        high, low = load(after(eigvecs, *mine))
        far, places = whole, [(a, b) for _, a, b in pieces[1:]]
        for piece, sent in zip(pieces[1:], parts_of(after(mine[0], high), places)):
            far += [(step, piece, from_chip(sent, step)) for step in range(1, chips)]
        own = {k: [(mine[k], share, 0), (sib[k], share, 0)] for k in (0, 1)}
        segments = {k: [(0, 0, 0, share), (0, 1, 0, share)] for k in (0, 1)}
        for step, (block, a, b), _ in far:
            segments[block] += [(step, 0, a, b), (step, 1, a, b)]
        all_ones, all_zeros = list(own[1]), list(own[0])
        running, flying, done = {}, {}, {}

        def start(*names):
            for name in names:
                if name not in running:
                    continue
                try:
                    flying[name] = running[name].send(flying.pop(name, None))
                except StopIteration as end:
                    done[name] = end.value
                    del running[name]

        def arrived(*names):
            return [flying[name] for name in names if name in flying]

        keep, send = project("project_own1", own[1], own[0], high, low, bit)
        running["own1"] = sums(keep, send)
        start("own1")
        front = project("project_own0", own[0], [], after(high, keep), low, bit)
        running["own0"] = sums(*front)
        start("own0")
        t0, t1 = reorder(where, after(factors, *front), share, chips, segments)
        front = (*front, t0)
        last = len(far) - 1
        for n, (step, (block, first, final), value) in enumerate(far):
            waits = list(running) if last != 2 else (("own1", "own0"), ("own1", 0, "own0"), ())[n]
            value = after(value, *front, *arrived(*waits))
            start(*waits if last != 2 else (("own1", "own0"), ("own1",), ())[n])
            split_rows = halves[block, first, final]
            pair = [(value, final - first, 0)]
            for at in range(0, final - first, swap_rows[block, first, final]):
                upto = min(at + swap_rows[block, first, final], final - first)
                pair.append((core_swap(value[at:upto]), upto - at, 0))
            ready = after(high, *arrived("own1")) if n == 2 and last == 2 else high
            if block == 1:
                all_ones += pair
                front = project(f"project_one_{n}", pair, own[0], high, low, bit if split_rows else None)
            else:
                all_zeros += pair
                front = project(f"project_zero_{n}", pair, all_ones, ready, low, bit if split_rows else None)
            running[n] = sums(*front)
            start(n)
            if n == 1 and last == 2:
                flying[0] = after(flying[0], *front)
                start(0)
        if last == 2:
            flying["own0"] = after(flying["own0"], *front)
            flying[last] = after(flying[last], *arrived(0))
            start("own0", 0)
        while running:
            start(*list(running))
        ones = [("own1", True)] + [(n, halves[f[1]]) for n, f in enumerate(far) if f[1][0] == 1]
        zeros = [("own0", True)] + [(n, halves[f[1]]) for n, f in enumerate(far) if f[1][0] == 0]
        ones_flat, zeros_flat = ([v for key, _ in group for v in done[key]] for group in (ones, zeros))

        def joined(where_ref, refs, group, columns):
            parts = []
            zero = where_ref[5] == 0
            for a, b, (_, chosen) in zip(refs[::2], refs[1::2], group):
                a, b = a[:, columns], b[:, columns]
                parts += [jnp.where(zero, a, b), jnp.where(zero, b, a)] if chosen else [a + b]
            return parts

        def make_one(where_ref, *refs):
            return jnp.concatenate(joined(where_ref, refs, ones, slice(0, nc)))

        def make_zero(where_ref, scaled_ref, *refs):
            ones_refs, zero_refs = refs[: len(ones_flat)], refs[len(ones_flat) :]
            scaled = scaled_ref[...]
            turned_gram = jnp.concatenate(joined(where_ref, ones_refs, ones, slice(nc, nc + half)))
            front = jnp.concatenate(joined(where_ref, zero_refs[:2], zeros[:1], slice(None)))
            later = jnp.concatenate(joined(where_ref, zero_refs[2:], zeros[1:], slice(None)))
            front -= short_dot(turned_gram, scaled, TN)
            return jnp.concatenate([front, later[:, :nc] - short_dot(later[:, nc:], scaled)])

        current, scaled = update("update_one", make_one, [bit, *ones_flat], t1, all_ones, [high, low], False)
        ins = [bit, scaled, *ones_flat, *zeros_flat]
        return update("update_zero", make_zero, ins, t0, all_zeros, [current], True)

    return local


def solution(mesh):
    placed = (P("groups", "col", "row"), P("groups", None, None), P(("groups", "row"), "col"))
    local = make_local(mesh.shape["col"] // 2, mesh.shape["row"])
    return jax.shard_map(
        local, mesh=mesh, in_specs=placed, out_specs=P(("groups", "row"), "col"), check_vma=False
    )
```

```python
import jax
import jax.numpy as jnp
from jax import lax
from jax.experimental import pallas as pl
from jax.experimental.pallas import tpu as pltpu
from jax.sharding import PartitionSpec as P

F32, BF16 = jnp.float32, jnp.bfloat16
PIECES = ((1, 0, 64, True), (0, 0, 40, True), (0, 40, 64, False))
SWAP_ROWS = (16, 16, 8)
NN = (((1,), (0,)), ((), ()))
NT = (((1,), (1,)), ((), ()))
TN = (((0,), (0,)), ((), ()))
SCALARS = pl.BlockSpec(memory_space=pltpu.SMEM)
VMEM = pl.BlockSpec(memory_space=pltpu.VMEM)
HBM = pl.BlockSpec(memory_space=pltpu.HBM)


def call(body, name, ins, specs, outs, out_specs, scratch=(), mib=8):
    return pl.pallas_call(
        body,
        in_specs=specs,
        out_specs=out_specs,
        out_shape=outs,
        scratch_shapes=list(scratch),
        compiler_params=pltpu.CompilerParams(vmem_limit_bytes=mib * 1024 * 1024),
        cost_estimate=pl.CostEstimate(flops=1, bytes_accessed=1, transcendentals=0),
        name=name,
    )(*ins)


def array(*shape, dtype=F32):
    return jax.ShapeDtypeStruct(shape, dtype)


def split(value):
    high = value.astype(BF16)
    return high, (value - high.astype(F32)).astype(BF16)


def dot(a, b, dims=NN):
    return lax.dot_general(a, b, dims, preferred_element_type=F32)


def full_dot(a, b, dims=NN):
    return lax.dot_general(a, b, dims, precision=lax.Precision.HIGHEST, preferred_element_type=F32)


def three(vh, vl, bh, bl, dims):
    rows = vh.shape[0]
    first = dot(jnp.concatenate([vh, vl]), bh, dims)
    return first[:rows] + first[rows:] + dot(vh, bl, dims)


def short_dot(a, b, dims=NN):
    (ah, al), (bh, bl) = split(a), split(b)
    return dot(ah, bh, dims) + dot(ah, bl, dims) + dot(al, bh, dims)


def steps_of(here, step):
    step = min(here, step)
    return [pl.ds(at, step) for at in range(0, here, step)]


def cut(where, vectors, width):
    _, share, here = vectors.shape
    strip = min(share, 16)
    strips = [(k, at) for k in (1, 0) for at in range(0, share, strip)]

    def body(where_ref, in_ref, zeros, ones, sems):
        outs = (zeros, ones)
        copies = []
        for n, (k, at) in enumerate(strips):
            ds = pl.ds(at, strip)
            copies.append(pltpu.make_async_copy(in_ref.at[k, ds], outs[k].at[ds], sems.at[n]))
            copies[-1].start()
        for copy, (k, at) in zip(copies, strips):
            copy.wait()
            shape = (strip, min(here, (k + 1) * width))
            along = lax.broadcasted_iota(jnp.int32, shape, 0) + (where_ref[0] + at + k * where_ref[2])
            across = lax.broadcasted_iota(jnp.int32, shape, 1) + where_ref[1]
            part = outs[k][at : at + strip, : shape[1]]
            outs[k][at : at + strip, : shape[1]] = jnp.where(across >= along, part, 0.0)

    sems = [pltpu.SemaphoreType.DMA((len(strips),))]
    return call(body, "cut", (where, vectors), [SCALARS, HBM], [array(share, here)] * 2, [VMEM] * 2, sems, 4)


def parts_of(mine, places):
    here = mine.shape[1]

    def body(in_ref, *refs):
        for (low, high), out in zip(places, refs):
            out[...] = in_ref[low:high]

    outs = [array(high - low, here) for low, high in places]
    return call(body, "parts", (mine,), [VMEM], outs, [VMEM] * len(outs), mib=2)


def load(eigvecs):
    here, nc = eigvecs.shape
    steps = steps_of(here, 512)

    def body(in_ref, high, low, held, sems):
        copies = [pltpu.make_async_copy(in_ref.at[ds], held.at[ds], sems.at[n]) for n, ds in enumerate(steps)]
        for copy in copies:
            copy.start()
        for copy, ds in zip(copies, steps):
            copy.wait()
            high[ds, :], low[ds, :] = split(held[ds, :])

    scratch = [pltpu.VMEM((here, nc), F32), pltpu.SemaphoreType.DMA((len(steps),))]
    return call(body, "load", (eigvecs,), [HBM], [array(here, nc, dtype=BF16)] * 2, [VMEM] * 2, scratch, 44)


def rows_of(refs, pieces, ds):
    return jnp.concatenate([ref[at : at + count, ds] for ref, (_, count, at) in zip(refs, pieces)])


def project(name, rows, partners, high, low, bit=None):
    here, nc = high.shape
    height = sum(count for _, count, _ in rows)
    extra = sum(count for _, count, _ in partners)
    steps = steps_of(here, 1024)

    def body(*refs):
        refs = list(refs)
        acc = refs.pop()
        bit_ref = refs.pop(0) if bit is not None else None
        row_refs, refs = refs[: len(rows)], refs[len(rows) :]
        partner_refs, refs = refs[: len(partners)], refs[len(partners) :]
        high_ref, low_ref = refs[:2]
        outs = refs[2:]
        for n, ds in enumerate(steps):
            vh, vl = split(rows_of(row_refs, rows, ds))
            main = three(vh, vl, high_ref[ds, :], low_ref[ds, :], NN)
            if partners:
                gram = three(vh, vl, *split(rows_of(partner_refs, partners, ds)), NT)
                main = jnp.concatenate([main, gram], axis=1)
            if n == 0:
                acc[...] = main
            else:
                acc[...] += main
        if bit is None:
            outs[0][...] = acc[...]
        else:
            half = height // 2
            zero = bit_ref[5] == 0
            outs[0][...] = jnp.where(zero, acc[:half], acc[half:])
            outs[1][...] = jnp.where(zero, acc[half:], acc[:half])

    outputs = 1 if bit is None else 2
    arrays = [r[0] for r in rows + partners] + [high, low]
    return call(
        body,
        name,
        ([] if bit is None else [bit]) + arrays,
        ([] if bit is None else [SCALARS]) + [VMEM] * len(arrays),
        [array(height // outputs, nc + extra)] * outputs,
        [VMEM] * outputs,
        [pltpu.VMEM((height, nc + extra), F32)],
    )


def reorder(where, factors, share, chips, segments):
    width = factors.shape[1]

    def body(where_ref, in_ref, *outs):
        chip, core = where_ref[3], where_ref[4]
        for block, out in enumerate(outs):
            picks = []
            for step, other, low, high in segments[block]:
                at = (lax.rem(chip + step, chips) * 2 + (core + other) % 2) * share + low
                shape = (high - low, width)
                same = lax.broadcasted_iota(jnp.int32, shape, 1) == lax.broadcasted_iota(jnp.int32, shape, 0) + at
                picks.append(jnp.where(same, 1.0, 0.0))
            pick = jnp.concatenate(picks)
            out[...] = full_dot(full_dot(pick, in_ref[block]), pick, NT)

    return call(body, "reorder", (where, factors), [SCALARS, VMEM], [array(width, width)] * 2, [VMEM] * 2)


def update(name, make, ins, factor, pieces, current, last):
    here, nc = current[0].shape
    width = factor.shape[0]
    steps = steps_of(here, 512)

    def body(*refs):
        in_refs, refs = refs[: len(ins)], refs[len(ins) :]
        factor_ref, refs = refs[0], refs[1:]
        piece_refs, refs = refs[: len(pieces)], refs[len(pieces) :]
        cur_refs, refs = refs[: len(current)], refs[len(current) :]
        out = refs[0]
        scaled = short_dot(factor_ref[...], make(*in_refs))
        sh, sl = split(scaled)
        if not last:
            refs[1][...] = scaled
        copies = []
        for n, ds in enumerate(steps):
            vh, vl = split(rows_of(piece_refs, pieces, ds))
            new = cur_refs[0][ds, :].astype(F32)
            for ref in cur_refs[1:]:
                new += ref[ds, :].astype(F32)
            new -= dot(vh, sh, TN) + dot(vh, sl, TN) + dot(vl, sh, TN)
            if last:
                held, sems = refs[1:]
                held[ds, :] = new
                copies.append(pltpu.make_async_copy(held.at[ds], out.at[ds], sems.at[n]))
                copies[-1].start()
            else:
                out[ds, :] = new
        for copy in copies:
            copy.wait()

    args = [*ins, factor, *[p[0] for p in pieces], *current]
    specs = [SCALARS if v.dtype == jnp.int32 else VMEM for v in args]
    if last:
        scratch = [pltpu.VMEM((here, nc), F32), pltpu.SemaphoreType.DMA((len(steps),))]
        return call(body, name, args, specs, array(here, nc), HBM, scratch, 13)
    return call(body, name, args, specs, [array(here, nc), array(width, nc)], [VMEM] * 2)


def make_local(chips, rows):
    cols = 2 * chips

    def core_swap(value):
        return lax.ppermute(value, "col", [(i, i ^ 1) for i in range(cols)])

    def from_chip(value, step):
        return lax.ppermute(value, "col", [((i + 2 * step) % cols, i) for i in range(cols)])

    def row_swap(value, step):
        return lax.ppermute(value, "row", [(i, i ^ step) for i in range(rows)])

    def sums(value, send=None):
        step, got = 1, None
        if send is not None:
            got = yield row_swap(send, 1)
            step = 2
        while step < rows:
            value = value if got is None else value + got
            got = yield row_swap(value, step)
            step *= 2
        if send is not None:
            value = value + got
            got = yield row_swap(value, 1)
        return value, got

    def local(vectors, factors, eigvecs):
        share, here = vectors.shape[1:]
        nc = eigvecs.shape[1]
        width = share * cols
        half = 2 * share
        col, row = lax.axis_index("col"), lax.axis_index("row")
        where = jnp.stack([col * share, row * here, jnp.int32(width), col // 2, col % 2, row % 2]).astype(jnp.int32)
        bit = where
        pieces = []
        for block, low, high, _ in PIECES:
            low, high = low * share // 64 // 8 * 8, high * share // 64 // 8 * 8
            pieces.append((block, low, high))
        swap_rows = dict(zip(pieces, SWAP_ROWS))
        halves = {piece: chosen for piece, (*_, chosen) in zip(pieces, PIECES)}

        def after(value, *others):
            return lax.optimization_barrier((value, *others))[0]

        mine = cut(where, vectors, width)
        whole = [(step, pieces[0], from_chip(mine[1], step)) for step in range(1, chips)]
        sib = [core_swap(m) for m in mine]
        high, low = load(after(eigvecs, *mine))
        far, places = whole, [(a, b) for _, a, b in pieces[1:]]
        for piece, sent in zip(pieces[1:], parts_of(after(mine[0], high), places)):
            far += [(step, piece, from_chip(sent, step)) for step in range(1, chips)]
        own = {k: [(mine[k], share, 0), (sib[k], share, 0)] for k in (0, 1)}
        segments = {k: [(0, 0, 0, share), (0, 1, 0, share)] for k in (0, 1)}
        for step, (block, a, b), _ in far:
            segments[block] += [(step, 0, a, b), (step, 1, a, b)]
        all_ones, all_zeros = list(own[1]), list(own[0])
        running, flying, done = {}, {}, {}

        def start(*names):
            for name in names:
                if name not in running:
                    continue
                try:
                    flying[name] = running[name].send(flying.pop(name, None))
                except StopIteration as end:
                    done[name] = end.value
                    del running[name]

        def arrived(*names):
            return [flying[name] for name in names if name in flying]

        keep, send = project("project_own1", own[1], own[0], high, low, bit)
        running["own1"] = sums(keep, send)
        start("own1")
        front = project("project_own0", own[0], [], after(high, keep), low, bit)
        running["own0"] = sums(*front)
        start("own0")
        t0, t1 = reorder(where, after(factors, *front), share, chips, segments)
        front = (*front, t0)
        last = len(far) - 1
        for n, (step, (block, first, final), value) in enumerate(far):
            waits = list(running) if last != 2 else (("own1", "own0"), ("own1", 0, "own0"), ())[n]
            value = after(value, *front, *arrived(*waits))
            start(*waits if last != 2 else (("own1", "own0"), ("own1",), ())[n])
            split_rows = halves[block, first, final]
            pair = [(value, final - first, 0)]
            for at in range(0, final - first, swap_rows[block, first, final]):
                upto = min(at + swap_rows[block, first, final], final - first)
                pair.append((core_swap(value[at:upto]), upto - at, 0))
            ready = after(high, *arrived("own1")) if n == 2 and last == 2 else high
            if block == 1:
                all_ones += pair
                front = project(f"project_one_{n}", pair, own[0], high, low, bit if split_rows else None)
            else:
                all_zeros += pair
                front = project(f"project_zero_{n}", pair, all_ones, ready, low, bit if split_rows else None)
            running[n] = sums(*front)
            start(n)
            if n == 1 and last == 2:
                flying[0] = after(flying[0], *front)
                start(0)
        if last == 2:
            flying["own0"] = after(flying["own0"], *front)
            flying[last] = after(flying[last], *arrived(0))
            start("own0", 0)
        while running:
            start(*list(running))
        ones = [("own1", True)] + [(n, halves[f[1]]) for n, f in enumerate(far) if f[1][0] == 1]
        zeros = [("own0", True)] + [(n, halves[f[1]]) for n, f in enumerate(far) if f[1][0] == 0]
        ones_flat, zeros_flat = ([v for key, _ in group for v in done[key]] for group in (ones, zeros))

        def joined(where_ref, refs, group, columns):
            parts = []
            zero = where_ref[5] == 0
            for a, b, (_, chosen) in zip(refs[::2], refs[1::2], group):
                a, b = a[:, columns], b[:, columns]
                parts += [jnp.where(zero, a, b), jnp.where(zero, b, a)] if chosen else [a + b]
            return parts

        def make_one(where_ref, *refs):
            return jnp.concatenate(joined(where_ref, refs, ones, slice(0, nc)))

        def make_zero(where_ref, scaled_ref, *refs):
            ones_refs, zero_refs = refs[: len(ones_flat)], refs[len(ones_flat) :]
            scaled = scaled_ref[...]
            turned_gram = jnp.concatenate(joined(where_ref, ones_refs, ones, slice(nc, nc + half)))
            front = jnp.concatenate(joined(where_ref, zero_refs[:2], zeros[:1], slice(None)))
            later = jnp.concatenate(joined(where_ref, zero_refs[2:], zeros[1:], slice(None)))
            front -= short_dot(turned_gram, scaled, TN)
            return jnp.concatenate([front, later[:, :nc] - short_dot(later[:, nc:], scaled)])

        current, scaled = update("update_one", make_one, [bit, *ones_flat], t1, all_ones, [high, low], False)
        ins = [bit, scaled, *ones_flat, *zeros_flat]
        return update("update_zero", make_zero, ins, t0, all_zeros, [current], True)

    return local


def solution(mesh):
    placed = (P("groups", "col", "row"), P("groups", None, None), P(("groups", "row"), "col"))
    local = make_local(mesh.shape["col"] // 2, mesh.shape["row"])
    return jax.shard_map(
        local, mesh=mesh, in_specs=placed, out_specs=P(("groups", "row"), "col"), check_vma=False
    )
```
